128 devices in a mesh: head: 4 (over z), tok: 32 (over y, x, core).
Axes of the slice: x: 4, y: 4, z: 4, core: 2. Of those that a mesh axis runs over, the one named last changes fastest.
Arguments:
- query_tokens: bfloat16 [16384, 2048], P(('head', 'tok')), may hold values from -6 to 6
- key_tokens: bfloat16 [16384, 2048], P(('head', 'tok')), may hold values from -6 to 6
- value_tokens: bfloat16 [16384, 2048], P(('head', 'tok')), may hold values from -6 to 6
- step_sizes: bfloat16 [16384, 8], P(('head', 'tok')), may hold values from 0.00049972534 to 0.0049743652
- fast_weights: float32 [8, 3, 512, 256], P('head'), may hold values from -0.375 to 0.375
- out_grad: bfloat16 [16384, 2048], P(('head', 'tok')), may hold values from -6 to 6
Outputs:
- meta_grad: float32 [8, 3, 512, 256], P('head', None, 'tok')
- query_grad: bfloat16 [16384, 2048], P(('head', 'tok'))
- key_grad: bfloat16 [16384, 2048], P(('head', 'tok'))
- value_grad: bfloat16 [16384, 2048], P(('head', 'tok'))
- step_grad: bfloat16 [16384, 8], P(('head', 'tok'))
The draws below stay inside these ranges and needn't reach their ends.
All inputs are finite; a program needn't handle non-finite values.
Results may differ from the reference program's by a relative error of at most 0.006.
Values may be sent and summed in bfloat16 or wider, within the bound.
No kernel may reach another device: no remote copies, remote signals or barrier semaphores. Data moves between devices by JAX's collectives and lax.ppermute only.
A program may use at most 128 MiB of HBM per device.

```python
import math
import jax
import jax.numpy as jnp
from jax import lax

HD = 256
HID = 512
HEADS = 8
TOKENS = 16384


def steps_of(stream_key, extent, cuts, smallest, high):
    level, own = 1.0, jax.random.fold_in(stream_key, 6)
    for dim, parts in cuts:
        heights = jnp.exp(jax.random.uniform(jax.random.fold_in(own, dim), (parts,), jnp.float32, smallest / len(cuts), high / len(cuts)))
        level = level * jnp.repeat(heights, extent[dim] // parts).reshape([-1 if axis == dim else 1 for axis in range(len(extent))])
    return level


def bell_draw(stream_key, dims, scale, reach, cuts=(), dtype=jnp.bfloat16):
    drawn = scale * jax.random.normal(stream_key, dims, jnp.float32)
    if cuts:
        drawn = drawn * steps_of(stream_key, dims, cuts, -0.22, 0.18)
    return jnp.clip(drawn, -reach, reach).astype(dtype)


def setup_inputs(seed: int = 0) -> dict:
    key_of = jax.random.split(jax.random.key(seed), 7)
    query_tokens = bell_draw(key_of[0], (TOKENS, HEADS * HD), 1.0, 6.0, ((0, 128),))
    key_tokens = bell_draw(key_of[1], (TOKENS, HEADS * HD), 1.0, 6.0, ((0, 128),))
    value_tokens = bell_draw(key_of[2], (TOKENS, HEADS * HD), 1.0, 6.0, ((0, 128),))
    step_sizes = jnp.clip(jnp.exp(math.log(0.0049743652) - 2.2979944 * jax.random.uniform(key_of[3], (TOKENS, HEADS), jnp.float32) ** steps_of(key_of[3], (TOKENS, HEADS), ((0, 128),), -0.2, 0.2)), 0.00049972534, 0.0049743652).astype(jnp.bfloat16)
    fast_weights = bell_draw(key_of[4], (HEADS, 3, HID, HD), HD ** -0.5, 0.375, ((0, 4),), jnp.float32)
    out_grad = bell_draw(key_of[5], (TOKENS, HEADS * HD), 1.0, 6.0, ((0, 128),))
    return {"query_tokens": query_tokens, "key_tokens": key_tokens, "value_tokens": value_tokens, "step_sizes": step_sizes, "fast_weights": fast_weights, "out_grad": out_grad}


HIGHEST = lax.Precision.HIGHEST
EPSILON = 1e-05

def inner_grad(weights, key_rows, value_rows, rate_rows):
    gate_act = jnp.dot(key_rows, weights[0].T, precision=HIGHEST)
    up_act = jnp.dot(key_rows, weights[1].T, precision=HIGHEST)
    sigmoid_gate = jax.nn.sigmoid(gate_act)
    hidden = gate_act * sigmoid_gate * up_act
    target = rate_rows[:, None] * value_rows
    grad_down = jnp.dot(hidden.T, target, precision=HIGHEST)
    d_hidden = jnp.dot(target, weights[2].T, precision=HIGHEST)
    d_gate = d_hidden * up_act * sigmoid_gate * (1.0 + gate_act * (1.0 - sigmoid_gate))
    d_up = d_hidden * gate_act * sigmoid_gate
    grad_gate = jnp.dot(d_gate.T, key_rows, precision=HIGHEST)
    grad_up = jnp.dot(d_up.T, key_rows, precision=HIGHEST)
    return jnp.stack([grad_gate, grad_up, grad_down])

def renorm(weights, update):
    shifted = weights + update
    old_norm = jnp.sqrt(lax.optimization_barrier(jnp.sum(weights * weights, axis=-1, keepdims=True)) + EPSILON)
    new_norm = jnp.sqrt(lax.optimization_barrier(jnp.sum(shifted * shifted, axis=-1, keepdims=True)) + EPSILON)
    return shifted * (old_norm / new_norm)

def fast_apply(weights, query_rows):
    gate_act = jnp.dot(query_rows, weights[0].T, precision=HIGHEST)
    up_act = jnp.dot(query_rows, weights[1].T, precision=HIGHEST)
    return jnp.dot(jax.nn.silu(gate_act) * up_act, weights[2], precision=HIGHEST)

def layer_forward(weights, query_rows, key_rows, value_rows, rate_rows):
    return fast_apply(renorm(weights, inner_grad(weights, key_rows, value_rows, rate_rows)), query_rows)

def head_grads(inputs):
    weights, query_rows, key_rows, value_rows, rate_rows, cotangent = inputs
    unused, puller = jax.vjp(layer_forward, weights, query_rows, key_rows, value_rows, rate_rows)
    return puller(cotangent)

def split_heads(tensor):
    return tensor.reshape(TOKENS, HEADS, HD).transpose(1, 0, 2).astype(jnp.float32)

def join_heads(tensor):
    return tensor.transpose(1, 0, 2).reshape(TOKENS, HEADS * HD).astype(jnp.bfloat16)

def reference(query_tokens, key_tokens, value_tokens, step_sizes, fast_weights, out_grad):
    results = lax.map(head_grads, (fast_weights, split_heads(query_tokens), split_heads(key_tokens), split_heads(value_tokens), step_sizes.T.astype(jnp.float32), split_heads(out_grad)))
    meta_grad, query_grad, key_grad, value_grad, step_grad = results
    return (meta_grad, join_heads(query_grad), join_heads(key_grad), join_heads(value_grad), step_grad.T.astype(jnp.bfloat16))
```

```python
import functools

import jax
import jax.numpy as jnp
from jax import lax
from jax.experimental import pallas as pl
from jax.experimental.pallas import tpu as pltpu
from jax.sharding import Mesh
from jax.sharding import PartitionSpec as P

EPSILON = 1e-05
PAD = 16
STEPS = 2
F32 = jnp.float32
BF16 = jnp.bfloat16


def mm(left, right, contract=(1, 0)):
    return lax.dot_general(
        left, right, (((contract[0],), (contract[1],)), ((), ())), preferred_element_type=F32
    )


def halves(value):
    high = value.astype(BF16)
    return high, (value - high.astype(F32)).astype(BF16)


def call(kernel, out_shape, flops=0, size=4 << 20, **options):
    return pl.pallas_call(
        kernel,
        out_shape=out_shape,
        compiler_params=pltpu.CompilerParams(vmem_limit_bytes=48 << 20),
        cost_estimate=pl.CostEstimate(flops=flops, bytes_accessed=size, transcendentals=0),
        **options,
    )


def shape(dims, dtype):
    return jax.ShapeDtypeStruct(dims, dtype)


def eye(size):
    rows = lax.broadcasted_iota(jnp.int32, (size, size), 0)
    columns = lax.broadcasted_iota(jnp.int32, (size, size), 1)
    return (rows == columns).astype(F32).astype(BF16)


def pack_kv_kernel(key_ref, value_ref, rate_ref, out_ref):
    heads, _, width = out_ref.shape
    rows = key_ref.shape[0]
    rates = mm(rate_ref[...], eye(rows), (0, 0))
    for head in range(heads):
        columns = slice(head * width, (head + 1) * width)
        out_ref[head, :rows] = key_ref[:, columns]
        out_ref[head, rows : 2 * rows] = value_ref[:, columns]
        row = jnp.broadcast_to(rates[head : head + 1], (PAD, rows))
        out_ref[head, 2 * rows :] = jnp.concatenate([row] * (width // rows), axis=1).astype(BF16)


def pack_qg_kernel(query_ref, cotangent_ref, out_ref):
    heads, _, width = out_ref.shape
    rows = query_ref.shape[0]
    for head in range(heads):
        columns = slice(head * width, (head + 1) * width)
        out_ref[head, :rows] = query_ref[:, columns]
        out_ref[head, rows:] = cotangent_ref[:, columns]


def unpack_kv_kernel(in_ref, key_ref, value_ref, rate_ref):
    heads, _, width = in_ref.shape
    rows = key_ref.shape[0]
    rates = jnp.concatenate(
        [in_ref[head, 2 * rows :, :rows].astype(F32)[:1] for head in range(heads)], axis=0
    )
    rate_ref[...] = mm(eye(rows), rates.astype(BF16), (1, 1)).astype(BF16)
    for head in range(heads):
        columns = slice(head * width, (head + 1) * width)
        key_ref[:, columns] = in_ref[head, :rows]
        value_ref[:, columns] = in_ref[head, rows : 2 * rows]


def unpack_q_kernel(in_ref, query_ref):
    heads, _, width = in_ref.shape
    for head in range(heads):
        query_ref[:, head * width : (head + 1) * width] = in_ref[head]


def rows_of(message, start, count):
    part = message[:, start : start + count]
    return part.reshape(part.shape[0] * count, part.shape[2])


def rate_row(message, rows):
    return jnp.concatenate(
        [message[s, 2 * rows :, :rows].astype(F32)[:1] for s in range(message.shape[0])], axis=1
    )


def add_to(acc_ref, index, value):
    @pl.when(pl.program_id(0) == 0)
    def _():
        acc_ref[index] = value

    @pl.when(pl.program_id(0) != 0)
    def _():
        acc_ref[index] += value


def finish(acc_ref, out_ref):
    owners, _, share, width = out_ref.shape

    @pl.when(pl.program_id(0) == pl.num_programs(0) - 1)
    def _():
        for index in range(3):
            out_ref[:, index] = acc_ref[index].astype(BF16).reshape(owners, share, width)


def inner_kernel(rows, m_ref, wh_ref, wl_ref, a_ref, b_ref, d_ref, out_ref, acc_ref):
    message = m_ref[...]
    k, v = rows_of(message, 0, rows), rows_of(message, rows, rows)
    r = rate_row(message, rows)
    a = mm(wh_ref[0], k, (1, 1)) + mm(wl_ref[0], k, (1, 1))
    b = mm(wh_ref[1], k, (1, 1)) + mm(wl_ref[1], k, (1, 1))
    d = mm(wh_ref[2], v, (1, 1)) + mm(wl_ref[2], v, (1, 1))
    a_ref[...], b_ref[...], d_ref[...] = a, b, d
    s = jax.nn.sigmoid(a)
    sa = a * s
    dh = d * r
    hid_h, hid_l = halves(sa * b * r)
    add_to(acc_ref, 2, mm(hid_h, v) + mm(hid_l, v))
    du_h, du_l = halves(dh * sa)
    add_to(acc_ref, 1, mm(du_h, k) + mm(du_l, k))
    dg_h, dg_l = halves(dh * b * (s * (1.0 + a * (1.0 - s))))
    add_to(acc_ref, 0, mm(dg_h, k) + mm(dg_l, k))
    finish(acc_ref, out_ref)


def whole(ref, index):
    part = ref[:, index]
    return part.reshape(part.shape[0] * part.shape[1], part.shape[2])


def outer_kernel(rows, m_ref, n_ref, dq_ref, out_ref, acc_ref):
    message = m_ref[...]
    q, g = rows_of(message, 0, rows), rows_of(message, rows, rows)
    gate, up, down = whole(n_ref, 0), whole(n_ref, 1), whole(n_ref, 2)
    a, b, d = mm(gate, q, (1, 1)), mm(up, q, (1, 1)), mm(down, g, (1, 1))
    s = jax.nn.sigmoid(a)
    sa = a * s
    hid_h, hid_l = halves(sa * b)
    add_to(acc_ref, 2, mm(hid_h, g) + mm(hid_l, g))
    du_h, du_l = halves(d * sa)
    add_to(acc_ref, 1, mm(du_h, q) + mm(du_l, q))
    dg_h, dg_l = halves(d * b * (s * (1.0 + a * (1.0 - s))))
    add_to(acc_ref, 0, mm(dg_h, q) + mm(dg_l, q))
    finish(acc_ref, out_ref)
    dq = mm(gate, dg_h, (0, 0)) + mm(gate, dg_l, (0, 0)) + mm(up, du_h, (0, 0)) + mm(up, du_l, (0, 0))
    dq_ref[...] = dq.T.astype(BF16).reshape(dq_ref.shape)


def second_kernel(rows, m_ref, wh_ref, wl_ref, c_ref, a_ref, b_ref, d_ref, dm_ref, out_ref, acc_ref):
    message = m_ref[...]
    k, v = rows_of(message, 0, rows), rows_of(message, rows, rows)
    r = rate_row(message, rows)
    gate, up, down = whole(c_ref, 0), whole(c_ref, 1), whole(c_ref, 2)
    a, b, d = a_ref[...], b_ref[...], d_ref[...]
    big_a, big_b, e = mm(gate, k, (1, 1)), mm(up, k, (1, 1)), mm(down, v, (1, 1))
    s = jax.nn.sigmoid(a)
    sa = a * s
    ds = s * (1.0 + a * (1.0 - s))
    dds = s * (1.0 - s) * (2.0 + a * (1.0 - 2.0 * s))
    dh, er = d * r, e * r
    bds = b * ds
    hid = sa * b
    ddh = big_a * bds + big_b * sa
    d_rate = jnp.sum(hid * e + ddh * d, axis=0, keepdims=True)
    db_h, db_l = halves(er * sa + big_a * (dh * ds))
    da_h, da_l = halves((er * b + big_b * dh) * ds + big_a * (dh * b * dds))
    add_to(acc_ref, 0, mm(da_h, k) + mm(da_l, k))
    add_to(acc_ref, 1, mm(db_h, k) + mm(db_l, k))
    dr_h, dr_l = halves(ddh * r)
    add_to(acc_ref, 2, mm(dr_h, v) + mm(dr_l, v))
    finish(acc_ref, out_ref)
    hid_h, hid_l = halves(hid * r)
    dv = mm(down, hid_h, (0, 0)) + mm(down, hid_l, (0, 0))
    dv += mm(wh_ref[2], dr_h, (0, 0)) + mm(wh_ref[2], dr_l, (0, 0)) + mm(wl_ref[2], dr_h, (0, 0))
    dg_h, dg_l = halves(dh * bds)
    du_h, du_l = halves(dh * sa)
    dk = mm(gate, dg_h, (0, 0)) + mm(gate, dg_l, (0, 0)) + mm(up, du_h, (0, 0)) + mm(up, du_l, (0, 0))
    dk += mm(wh_ref[0], da_h, (0, 0)) + mm(wh_ref[0], da_l, (0, 0)) + mm(wl_ref[0], da_h, (0, 0))
    dk += mm(wh_ref[1], db_h, (0, 0)) + mm(wh_ref[1], db_l, (0, 0)) + mm(wl_ref[1], db_h, (0, 0))
    sources, _, width = dm_ref.shape
    dm_ref[:, :rows] = dk.T.astype(BF16).reshape(sources, rows, width)
    dm_ref[:, rows : 2 * rows] = dv.T.astype(BF16).reshape(sources, rows, width)
    for source in range(sources):
        row = jnp.broadcast_to(d_rate[:, source * rows : (source + 1) * rows], (PAD, rows))
        dm_ref[source, 2 * rows :] = jnp.concatenate([row] * (width // rows), axis=1).astype(BF16)


def total_of(in_ref):
    total = in_ref[0].astype(F32)
    for source in range(1, in_ref.shape[0]):
        total += in_ref[source].astype(F32)
    return total


def norm_of(rows):
    return jnp.sqrt(jnp.sum(rows * rows, axis=-1, keepdims=True) + EPSILON)


def spread(value, out_ref):
    rounded = value.astype(BF16)
    for owner in range(out_ref.shape[0]):
        out_ref[owner] = rounded


def update_kernel(in_ref, w_ref, out_ref, moved_ref):
    w = w_ref[...]
    moved = w + total_of(in_ref)
    moved_ref[...] = moved
    spread(moved * (norm_of(w) / norm_of(moved)), out_ref)


def back_kernel(in_ref, w_ref, moved_ref, out_ref, direct_ref):
    w, moved = w_ref[...], moved_ref[...]
    given = total_of(in_ref)
    old, new = norm_of(w), norm_of(moved)
    along = jnp.sum(given * moved, axis=-1, keepdims=True) / new
    cotangent = (given - moved * (along / new)) * (old / new)
    direct_ref[...] = cotangent + w * (along / old)
    spread(cotangent, out_ref)


def last_kernel(in_ref, direct_ref, out_ref):
    out_ref[...] = total_of(in_ref) + direct_ref[...]


def body(query_tokens, key_tokens, value_tokens, step_sizes, fast_weights, out_grad):
    rows = query_tokens.shape[0]
    heads = lax.axis_size("z") * lax.axis_size("c")
    owners = lax.axis_size("p")
    width = query_tokens.shape[1] // heads
    hid = fast_weights.shape[2]
    share = hid // owners
    place, core = lax.axis_index("p"), lax.axis_index("c")
    steps = STEPS
    group = heads // steps
    tokens = group * rows
    product = 2 * heads * rows * hid * width

    def swap(message):
        return lax.all_to_all(message, ("z", "c"), 0, 0, tiled=True)

    def scatter(message):
        message = message.reshape(owners, 3 * share, width)
        return lax.all_to_all(message, "p", 0, 0, tiled=True)

    weights = lax.dynamic_index_in_dim(fast_weights, core, 0, keepdims=False)
    own = lax.dynamic_slice_in_dim(weights, place * share, share, 1).reshape(3 * share, width)
    rounded = lax.reduce_precision(weights, 8, 7)
    w_high, w_low = rounded.astype(BF16), (weights - rounded).astype(BF16)

    kv = swap(
        call(pack_kv_kernel, shape((heads, 2 * rows + PAD, width), BF16))(
            key_tokens, value_tokens, step_sizes
        )
    )
    qg = swap(call(pack_qg_kernel, shape((heads, 2 * rows, width), BF16))(query_tokens, out_grad))

    def blocks(count):
        return pl.BlockSpec((group, count, width), lambda i: (i, 0, 0))

    def full(*dims):
        return pl.BlockSpec(dims, lambda i: (0,) * len(dims))

    activation = pl.BlockSpec((hid, tokens), lambda i: (0, i))
    parts = full(owners, 3, share, width)
    part_shape = shape((owners, 3, share, width), BF16)
    act_shape = shape((hid, heads * rows), F32)
    scratch = [pltpu.VMEM((3, hid, width), F32)]
    a, b, d, grad_part = call(
        functools.partial(inner_kernel, rows),
        (act_shape, act_shape, act_shape, part_shape),
        flops=12 * product,
        grid=(steps,),
        in_specs=[blocks(2 * rows + PAD), full(3, hid, width), full(3, hid, width)],
        out_specs=[activation, activation, activation, parts],
        scratch_shapes=scratch,
    )(kv, w_high, w_low)
    own_shape = shape((3 * share, width), F32)
    spread_shape = shape((owners, 3 * share, width), BF16)
    updated, moved = call(update_kernel, (spread_shape, own_shape))(scatter(grad_part), own)
    updated = scatter(updated).reshape(owners, 3, share, width)
    d_queries, d_part = call(
        functools.partial(outer_kernel, rows),
        (shape((heads, rows, width), BF16), part_shape),
        flops=13 * product,
        grid=(steps,),
        in_specs=[blocks(2 * rows), parts],
        out_specs=[blocks(rows), parts],
        scratch_shapes=scratch,
    )(qg, updated)
    cotangent, direct = call(back_kernel, (spread_shape, own_shape))(scatter(d_part), own, moved)
    cotangent = scatter(cotangent).reshape(owners, 3, share, width)
    d_kv, second_part = call(
        functools.partial(second_kernel, rows),
        (shape((heads, 2 * rows + PAD, width), BF16), part_shape),
        flops=24 * product,
        grid=(steps,),
        in_specs=[
            blocks(2 * rows + PAD),
            full(3, hid, width),
            full(3, hid, width),
            parts,
            activation,
            activation,
            activation,
        ],
        out_specs=[blocks(2 * rows + PAD), parts],
        scratch_shapes=scratch,
    )(kv, w_high, w_low, cotangent, a, b, d)
    wide = (rows, heads * width)
    query_grad = call(unpack_q_kernel, shape(wide, BF16))(swap(d_queries))
    key_grad, value_grad, step_grad = call(
        unpack_kv_kernel, (shape(wide, BF16), shape(wide, BF16), shape((rows, heads), BF16))
    )(swap(d_kv))
    summed = call(last_kernel, own_shape)(scatter(second_part), direct)
    summed = summed.reshape(3, 2, share // 2, width)
    kept = lax.dynamic_index_in_dim(summed, core, 1, keepdims=False)
    sent = lax.dynamic_index_in_dim(summed, 1 - core, 1, keepdims=False)
    got = lax.ppermute(sent, "c", [(0, 1), (1, 0)])
    first = core == 0
    meta_grad = jnp.stack([jnp.where(first, kept, got), jnp.where(first, got, kept)])
    return meta_grad, query_grad, key_grad, value_grad, step_grad


def solution(mesh):
    layers, lines = mesh.devices.shape
    small = Mesh(mesh.devices.reshape(layers, lines // 2, 2), ("z", "p", "c"))
    rows = P(("z", "p", "c"), None)
    return jax.shard_map(
        body,
        mesh=small,
        in_specs=(rows, rows, rows, rows, P("z", None, None, None), rows),
        out_specs=(P("z", None, ("p", "c"), None), rows, rows, rows, rows),
        check_vma=False,
    )
```

```python
import functools

import jax
import jax.numpy as jnp
from jax import lax
from jax.experimental import pallas as pl
from jax.experimental.pallas import tpu as pltpu
from jax.sharding import Mesh
from jax.sharding import PartitionSpec as P

EPSILON = 1e-05
PAD = 16
STEPS = 2
F32 = jnp.float32
BF16 = jnp.bfloat16


def mm(left, right, contract=(1, 0)):
    return lax.dot_general(
        left, right, (((contract[0],), (contract[1],)), ((), ())), preferred_element_type=F32
    )


def halves(value):
    high = value.astype(BF16)
    return high, (value - high.astype(F32)).astype(BF16)


def call(kernel, out_shape, flops=0, size=4 << 20, vmem=8, **options):
    return pl.pallas_call(
        kernel,
        out_shape=out_shape,
        compiler_params=pltpu.CompilerParams(vmem_limit_bytes=vmem << 20),
        cost_estimate=pl.CostEstimate(flops=flops, bytes_accessed=size, transcendentals=0),
        **options,
    )


def shape(dims, dtype):
    return jax.ShapeDtypeStruct(dims, dtype)


def mask_row(dims, index):
    return lax.broadcasted_iota(jnp.int32, dims, 0) == index


def padded_row(row, width):
    block = jnp.broadcast_to(row, (PAD, row.shape[1]))
    return jnp.concatenate([block] * (width // row.shape[1]), axis=1).astype(BF16)


def columns_of(place_ref, slot, width):
    return pl.ds(pl.multiple_of(place_ref[slot] * width, width), width)


def pieces(own_refs, got_refs):
    half = own_refs[0].shape[0] // 2
    return [ref.at[:half] for ref in own_refs] + [ref.at[half:] for ref in got_refs]


def pack_kv_kernel(place_ref, key_ref, value_ref, rate_ref, *out_refs):
    rows, width = key_ref.shape[0], out_refs[0].shape[1]
    rates = rate_ref[...].astype(F32)
    for slot, out_ref in enumerate(pieces(out_refs, out_refs)):
        columns = columns_of(place_ref, slot, width)
        out_ref[:rows] = key_ref[:, columns]
        out_ref[rows : 2 * rows] = value_ref[:, columns]
        chosen = jnp.where(mask_row(rates.shape, place_ref[slot]), rates, 0.0)
        out_ref[2 * rows :] = padded_row(jnp.sum(chosen, axis=0, keepdims=True), width)


def pack_qg_kernel(place_ref, query_ref, cotangent_ref, *out_refs):
    rows, width = query_ref.shape[0], out_refs[0].shape[1]
    for slot, out_ref in enumerate(pieces(out_refs, out_refs)):
        columns = columns_of(place_ref, slot, width)
        out_ref[:rows] = query_ref[:, columns]
        out_ref[rows:] = cotangent_ref[:, columns]


def unpack_kv_kernel(place_ref, *refs):
    in_refs, (key_ref, value_ref, rate_ref) = refs[:-3], refs[-3:]
    rows, width = key_ref.shape[0], in_refs[0].shape[1]
    count = len(in_refs) // 2
    rates = jnp.zeros(rate_ref.shape, F32)
    for slot, in_ref in enumerate(pieces(in_refs[:count], in_refs[count:])):
        columns = columns_of(place_ref, slot, width)
        key_ref[:, columns] = in_ref[:rows]
        value_ref[:, columns] = in_ref[rows : 2 * rows]
        row = in_ref[2 * rows :, :rows].astype(F32)[:1]
        rates = jnp.where(mask_row(rates.shape, place_ref[slot]), row, rates)
    rate_ref[...] = rates.astype(BF16)


def unpack_q_kernel(place_ref, *refs):
    in_refs, query_ref = refs[:-1], refs[-1]
    width, count = in_refs[0].shape[1], len(in_refs) // 2
    for slot, in_ref in enumerate(pieces(in_refs[:count], in_refs[count:])):
        query_ref[:, columns_of(place_ref, slot, width)] = in_ref[...]


def rows_of(refs, start, count):
    return jnp.concatenate([ref[start : start + count] for ref in refs], axis=0)


def rate_row(refs, rows):
    return jnp.concatenate([ref[2 * rows :, :rows].astype(F32)[:1] for ref in refs], axis=1)


def groups_of(refs):
    size = len(refs) // STEPS
    return [(step, refs[step * size : (step + 1) * size]) for step in range(STEPS)]


def start_all(pairs, sem_ref, first=0):
    copies = [
        pltpu.make_async_copy(source, target, sem_ref.at[first + number])
        for number, (source, target) in enumerate(pairs)
    ]
    for copy in copies:
        copy.start()
    return copies


def add_to(acc_ref, out_ref, step, index, value):
    owners, _, share, width = out_ref.shape
    if step:
        value = acc_ref[index] + value
    if step < STEPS - 1:
        acc_ref[index] = value
    else:
        out_ref[:, index] = value.astype(BF16).reshape(owners, share, width)


def inner_kernel(rows, *refs):
    sources, (wh_ref, wl_ref, act_ref, out_ref, acc_ref, held_ref, sem_ref) = refs[:-7], refs[-7:]
    messages = pieces(sources[: len(sources) // 2], sources[len(sources) // 2 :])
    copies = []
    for step, group in groups_of(messages):
        put = functools.partial(add_to, acc_ref, out_ref, step)
        k, v = rows_of(group, 0, rows), rows_of(group, rows, rows)
        r = rate_row(group, rows)
        a = mm(wh_ref[0], k, (1, 1)) + mm(wl_ref[0], k, (1, 1))
        b = mm(wh_ref[1], k, (1, 1)) + mm(wl_ref[1], k, (1, 1))
        d = mm(wh_ref[2], v, (1, 1)) + mm(wl_ref[2], v, (1, 1))
        held_ref[step, 0], held_ref[step, 1], held_ref[step, 2] = a, b, d
        copies += start_all([(held_ref.at[step], act_ref.at[step])], sem_ref, step)
        s = jax.nn.sigmoid(a)
        sa = a * s
        dh = d * r
        hid_h, hid_l = halves(sa * b * r)
        put(2, mm(hid_h, v) + mm(hid_l, v))
        du_h, du_l = halves(dh * sa)
        put(1, mm(du_h, k) + mm(du_l, k))
        dg_h, dg_l = halves(dh * b * (s * (1.0 + a * (1.0 - s))))
        put(0, mm(dg_h, k) + mm(dg_l, k))
    for copy in copies:
        copy.wait()


def whole(ref, index):
    part = ref[:, index]
    return part.reshape(part.shape[0] * part.shape[1], part.shape[2])


def give(refs, value, start, rows):
    rounded = value.T.astype(BF16)
    for slot, ref in enumerate(refs):
        ref[start : start + rows] = rounded[slot * rows : (slot + 1) * rows]


def outer_kernel(rows, *refs):
    layers = (len(refs) - 5) // 3
    messages, n_ref = pieces(refs[:layers], refs[layers : 2 * layers]), refs[2 * layers]
    gifts, (out_ref, acc_ref, held_ref, sem_ref) = refs[2 * layers + 1 : -4], refs[-4:]
    gifts = pieces(gifts, gifts)
    copies = []
    gate, up, down = whole(n_ref, 0), whole(n_ref, 1), whole(n_ref, 2)
    for (step, group), (_, back) in zip(groups_of(messages), groups_of(gifts)):
        put = functools.partial(add_to, acc_ref, out_ref, step)
        q, g = rows_of(group, 0, rows), rows_of(group, rows, rows)
        a, b, d = mm(gate, q, (1, 1)), mm(up, q, (1, 1)), mm(down, g, (1, 1))
        s = jax.nn.sigmoid(a)
        sa = a * s
        hid_h, hid_l = halves(sa * b)
        put(2, mm(hid_h, g) + mm(hid_l, g))
        du_h, du_l = halves(d * sa)
        put(1, mm(du_h, q) + mm(du_l, q))
        dg_h, dg_l = halves(d * b * (s * (1.0 + a * (1.0 - s))))
        put(0, mm(dg_h, q) + mm(dg_l, q))
        dq = mm(gate, dg_h, (0, 0)) + mm(gate, dg_l, (0, 0))
        dq += mm(up, du_h, (0, 0)) + mm(up, du_l, (0, 0))
        held = [held_ref.at[step * len(back) + slot] for slot in range(len(back))]
        give(held, dq, 0, rows)
        copies += start_all(list(zip(held, back)), sem_ref, step * len(back))
    for copy in copies:
        copy.wait()


def second_kernel(rows, *refs):
    layers = (len(refs) - 12) // 3
    sources = pieces(refs[:layers], refs[layers : 2 * layers])
    wh_ref, wl_ref, c_ref, stored_ref = refs[2 * layers : 2 * layers + 4]
    gifts, rest = refs[2 * layers + 4 : -8], refs[-8:]
    gifts = pieces(gifts, gifts)
    out_ref, acc_ref, message_ref, act_ref, held_ref, message_sem, act_sem, held_sem = rest
    messages = [message_ref.at[slot] for slot in range(len(sources))]
    loads = start_all(list(zip(sources, messages)), message_sem)
    act_loads = start_all([(stored_ref.at[step], act_ref.at[step]) for step in range(STEPS)], act_sem)
    copies = []
    gate, up, down = whole(c_ref, 0), whole(c_ref, 1), whole(c_ref, 2)
    for (step, group), (_, back) in zip(groups_of(messages), groups_of(gifts)):
        put = functools.partial(add_to, acc_ref, out_ref, step)
        for load in loads[step * len(group) : (step + 1) * len(group)]:
            load.wait()
        k, v = rows_of(group, 0, rows), rows_of(group, rows, rows)
        r = rate_row(group, rows)
        big_a, big_b, e = mm(gate, k, (1, 1)), mm(up, k, (1, 1)), mm(down, v, (1, 1))
        act_loads[step].wait()
        a, b, d = act_ref[step, 0], act_ref[step, 1], act_ref[step, 2]
        s = jax.nn.sigmoid(a)
        sa = a * s
        ds = s * (1.0 + a * (1.0 - s))
        dds = s * (1.0 - s) * (2.0 + a * (1.0 - 2.0 * s))
        dh, er = d * r, e * r
        bds = b * ds
        hid = sa * b
        ddh = big_a * bds + big_b * sa
        d_rate = jnp.sum(hid * e + ddh * d, axis=0, keepdims=True)
        db_h, db_l = halves(er * sa + big_a * (dh * ds))
        da_h, da_l = halves((er * b + big_b * dh) * ds + big_a * (dh * b * dds))
        put(0, mm(da_h, k) + mm(da_l, k))
        put(1, mm(db_h, k) + mm(db_l, k))
        dr_h, dr_l = halves(ddh * r)
        put(2, mm(dr_h, v) + mm(dr_l, v))
        hid_h, hid_l = halves(hid * r)
        dv = mm(down, hid_h, (0, 0)) + mm(down, hid_l, (0, 0))
        dv += mm(wh_ref[2], dr_h, (0, 0)) + mm(wh_ref[2], dr_l, (0, 0)) + mm(wl_ref[2], dr_h, (0, 0))
        dg_h, dg_l = halves(dh * bds)
        du_h, du_l = halves(dh * sa)
        dk = mm(gate, dg_h, (0, 0)) + mm(gate, dg_l, (0, 0))
        dk += mm(up, du_h, (0, 0)) + mm(up, du_l, (0, 0))
        dk += mm(wh_ref[0], da_h, (0, 0)) + mm(wh_ref[0], da_l, (0, 0)) + mm(wl_ref[0], da_h, (0, 0))
        dk += mm(wh_ref[1], db_h, (0, 0)) + mm(wh_ref[1], db_l, (0, 0)) + mm(wl_ref[1], db_h, (0, 0))
        held = [held_ref.at[step * len(back) + slot] for slot in range(len(back))]
        give(held, dk, 0, rows)
        give(held, dv, rows, rows)
        for slot, ref in enumerate(held):
            ref[2 * rows :] = padded_row(d_rate[:, slot * rows : (slot + 1) * rows], ref.shape[1])
        copies += start_all(list(zip(held, back)), held_sem, step * len(back))
    for copy in copies:
        copy.wait()


def total_of(in_ref):
    total = in_ref[0].astype(F32)
    for source in range(1, in_ref.shape[0]):
        total += in_ref[source].astype(F32)
    return total


def norm_of(rows):
    return jnp.sqrt(jnp.sum(rows * rows, axis=-1, keepdims=True) + EPSILON)


def spread(value, out_ref):
    rounded = value.astype(BF16)
    for owner in range(out_ref.shape[0]):
        out_ref[owner] = rounded


def update_kernel(in_ref, w_ref, out_ref, moved_ref):
    w = w_ref[...]
    moved = w + total_of(in_ref)
    moved_ref[...] = moved
    spread(moved * (norm_of(w) / norm_of(moved)), out_ref)


def back_kernel(in_ref, w_ref, moved_ref, out_ref, direct_ref):
    w, moved = w_ref[...], moved_ref[...]
    given = total_of(in_ref)
    old, new = norm_of(w), norm_of(moved)
    along = jnp.sum(given * moved, axis=-1, keepdims=True) / new
    cotangent = (given - moved * (along / new)) * (old / new)
    direct_ref[...] = cotangent + w * (along / old)
    spread(cotangent, out_ref)


def last_kernel(in_ref, direct_ref, out_ref):
    out_ref[...] = total_of(in_ref) + direct_ref[...]


def body(query_tokens, key_tokens, value_tokens, step_sizes, fast_weights, out_grad):
    rows = query_tokens.shape[0]
    layers, cores = lax.axis_size("z"), lax.axis_size("c")
    heads = layers * cores
    owners = lax.axis_size("p")
    width = query_tokens.shape[1] // heads
    hid = fast_weights.shape[2]
    share = hid // owners
    layer, place, core = lax.axis_index("z"), lax.axis_index("p"), lax.axis_index("c")
    product = 2 * heads * rows * hid * width
    shifts = [0, layers // 2] + [up for up in range(1, layers) if up != layers // 2]
    places = jnp.stack(
        [(layer + up) % layers * cores + (core + over) % cores for over in range(cores) for up in shifts]
    ).astype(jnp.int32)

    def along(messages, sign):
        pairs = [[(z, (z + sign * up) % layers) for z in range(layers)] for up in shifts]
        moved = [lax.ppermute(m, "z", pair) for m, pair in zip(messages[1:], pairs[1:])]
        return [messages[0]] + moved

    def across(messages):
        return [lax.ppermute(message, "c", [(0, 1), (1, 0)]) for message in messages]

    def scatter(message):
        message = message.reshape(owners, 3 * share, width)
        return lax.all_to_all(message, "p", 0, 0, tiled=True)

    weights = lax.dynamic_index_in_dim(fast_weights, core, 0, keepdims=False)
    own = lax.dynamic_slice_in_dim(weights, place * share, share, 1).reshape(3 * share, width)
    rounded = lax.reduce_precision(weights, 8, 7)
    w_high, w_low = rounded.astype(BF16), (weights - rounded).astype(BF16)
    memory = pl.BlockSpec(memory_space=pltpu.VMEM)
    scalars = pl.BlockSpec(memory_space=pltpu.SMEM)

    def messages_of(count):
        return (shape((cores * count, width), BF16),) * layers

    kv = along(
        call(
            pack_kv_kernel, messages_of(2 * rows + PAD), in_specs=[scalars, memory, memory, memory]
        )(places, key_tokens, value_tokens, step_sizes.T),
        1,
    )
    kv += across(kv)
    qg = along(
        call(pack_qg_kernel, messages_of(2 * rows), in_specs=[scalars, memory, memory])(
            places, query_tokens, out_grad
        ),
        1,
    )
    part_shape = shape((owners, 3, share, width), BF16)
    act_dims = (STEPS, 3, hid, heads * rows // STEPS)
    scratch = [pltpu.VMEM((3, hid, width), F32)]
    main = pl.BlockSpec(memory_space=pltpu.HBM)
    acts, grad_part = call(
        functools.partial(inner_kernel, rows),
        (shape(act_dims, F32), part_shape),
        flops=12 * product,
        vmem=60,
        in_specs=[memory] * (heads + 2),
        out_specs=[main, memory],
        scratch_shapes=scratch + [pltpu.VMEM(act_dims, F32), pltpu.SemaphoreType.DMA((STEPS,))],
    )(*kv, w_high, w_low)
    own_shape = shape((3 * share, width), F32)
    spread_shape = shape((owners, 3 * share, width), BF16)
    summed, qg = lax.optimization_barrier((scatter(grad_part), qg))
    updated, moved = call(update_kernel, (spread_shape, own_shape))(summed, own)
    updated, got = lax.optimization_barrier((scatter(updated), across(qg)))
    updated, qg = updated.reshape(owners, 3, share, width), qg + got
    *d_queries, d_part = call(
        functools.partial(outer_kernel, rows),
        messages_of(rows) + (part_shape,),
        flops=13 * product,
        vmem=60,
        in_specs=[memory] * (heads + 1),
        out_specs=[main] * layers + [memory],
        scratch_shapes=scratch
        + [pltpu.VMEM((heads, rows, width), BF16), pltpu.SemaphoreType.DMA((heads,))],
    )(*qg, updated)
    given, d_queries = lax.optimization_barrier((scatter(d_part), along(d_queries, -1)))
    cotangent, direct = call(back_kernel, (spread_shape, own_shape))(given, own, moved)
    wide = (rows, heads * width)
    taken = [scalars] + [memory] * heads
    query_grad = call(unpack_q_kernel, shape(wide, BF16), in_specs=taken)(
        places, *d_queries, *across(d_queries)
    )
    cotangent, query_grad = lax.optimization_barrier((scatter(cotangent), query_grad))
    cotangent = cotangent.reshape(owners, 3, share, width)
    *d_kv, second_part = call(
        functools.partial(second_kernel, rows),
        messages_of(2 * rows + PAD) + (part_shape,),
        flops=24 * product,
        vmem=60,
        in_specs=[main] * heads + [memory] * 3 + [main],
        out_specs=[main] * layers + [memory],
        scratch_shapes=scratch
        + [
            pltpu.VMEM((heads, 2 * rows + PAD, width), BF16),
            pltpu.VMEM(act_dims, F32),
            pltpu.VMEM((heads, 2 * rows + PAD, width), BF16),
            pltpu.SemaphoreType.DMA((heads,)),
            pltpu.SemaphoreType.DMA((STEPS,)),
            pltpu.SemaphoreType.DMA((heads,)),
        ],
    )(*kv, w_high, w_low, cotangent, acts)
    d_kv = along(d_kv, -1)
    key_grad, value_grad, step_grad = call(
        unpack_kv_kernel,
        (shape(wide, BF16), shape(wide, BF16), shape((heads, rows), BF16)),
        in_specs=taken,
    )(places, *d_kv, *across(d_kv))
    step_grad = step_grad.T
    summed = call(last_kernel, own_shape)(scatter(second_part), direct)
    summed = summed.reshape(3, 2, share // 2, width)
    kept = lax.dynamic_index_in_dim(summed, core, 1, keepdims=False)
    sent = lax.dynamic_index_in_dim(summed, 1 - core, 1, keepdims=False)
    got = lax.ppermute(sent, "c", [(0, 1), (1, 0)])
    first = core == 0
    meta_grad = jnp.stack([jnp.where(first, kept, got), jnp.where(first, got, kept)])
    return meta_grad, query_grad, key_grad, value_grad, step_grad


def solution(mesh):
    layers, lines = mesh.devices.shape
    small = Mesh(mesh.devices.reshape(layers, lines // 2, 2), ("z", "p", "c"))
    rows = P(("z", "p", "c"), None)
    return jax.shard_map(
        body,
        mesh=small,
        in_specs=(rows, rows, rows, rows, P("z", None, None, None), rows),
        out_specs=(P("z", None, ("p", "c"), None), rows, rows, rows, rows),
        check_vma=False,
    )
```

```python
import functools

import jax
import jax.numpy as jnp
from jax import lax
from jax.experimental import pallas as pl
from jax.experimental.pallas import tpu as pltpu
from jax.sharding import Mesh
from jax.sharding import PartitionSpec as P

EPSILON = 1e-05
PAD = 16
STEPS = 2
ROW_BLOCK = 16
COLUMN_BLOCK = 256
F32 = jnp.float32
BF16 = jnp.bfloat16


def mm(left, right, contract=(1, 0)):
    return lax.dot_general(
        left, right, (((contract[0],), (contract[1],)), ((), ())), preferred_element_type=F32
    )


def halves(value):
    high = value.astype(BF16)
    return high, (value - high.astype(F32)).astype(BF16)


def call(kernel, out_shape, flops=0, size=4 << 20, vmem=8, **options):
    return pl.pallas_call(
        kernel,
        out_shape=out_shape,
        compiler_params=pltpu.CompilerParams(vmem_limit_bytes=vmem << 20),
        cost_estimate=pl.CostEstimate(flops=flops, bytes_accessed=size, transcendentals=0),
        **options,
    )


def shape(dims, dtype):
    return jax.ShapeDtypeStruct(dims, dtype)


def mask_row(dims, index):
    return lax.broadcasted_iota(jnp.int32, dims, 0) == index


def padded_row(row, width):
    block = jnp.broadcast_to(row, (PAD, row.shape[1]))
    return jnp.concatenate([block] * (width // row.shape[1]), axis=1).astype(BF16)


def columns_of(place_ref, slot, width):
    return pl.ds(pl.multiple_of(place_ref[slot] * width, width), width)


def pieces(own_refs, got_refs):
    half = own_refs[0].shape[0] // 2
    return [ref.at[:half] for ref in own_refs] + [ref.at[half:] for ref in got_refs]


def pack_kv_kernel(place_ref, key_ref, value_ref, rate_ref, *out_refs):
    rows, width = key_ref.shape[0], out_refs[0].shape[1]
    rates = rate_ref[...].astype(F32)
    for slot, out_ref in enumerate(pieces(out_refs, out_refs)):
        columns = columns_of(place_ref, slot, width)
        out_ref[:rows] = key_ref[:, columns]
        out_ref[rows : 2 * rows] = value_ref[:, columns]
        chosen = jnp.where(mask_row(rates.shape, place_ref[slot]), rates, 0.0)
        out_ref[2 * rows :] = padded_row(jnp.sum(chosen, axis=0, keepdims=True), width)


def pack_qg_kernel(place_ref, query_ref, cotangent_ref, *out_refs):
    rows, width = query_ref.shape[0], out_refs[0].shape[1]
    for slot, out_ref in enumerate(pieces(out_refs, out_refs)):
        columns = columns_of(place_ref, slot, width)
        out_ref[:rows] = query_ref[:, columns]
        out_ref[rows:] = cotangent_ref[:, columns]


def unpack_kv_kernel(place_ref, *refs):
    in_refs, (key_ref, value_ref, rate_ref) = refs[:-3], refs[-3:]
    rows, width = key_ref.shape[0], in_refs[0].shape[1]
    count = len(in_refs) // 2
    rates = jnp.zeros(rate_ref.shape, F32)
    for slot, in_ref in enumerate(pieces(in_refs[:count], in_refs[count:])):
        columns = columns_of(place_ref, slot, width)
        key_ref[:, columns] = in_ref[:rows]
        value_ref[:, columns] = in_ref[rows : 2 * rows]
        row = in_ref[2 * rows :, :rows].astype(F32)[:1]
        rates = jnp.where(mask_row(rates.shape, place_ref[slot]), row, rates)
    rate_ref[...] = rates.astype(BF16)


def unpack_q_kernel(place_ref, *refs):
    in_refs, query_ref = refs[:-1], refs[-1]
    width, count = in_refs[0].shape[1], len(in_refs) // 2
    for slot, in_ref in enumerate(pieces(in_refs[:count], in_refs[count:])):
        query_ref[:, columns_of(place_ref, slot, width)] = in_ref[...]


def rows_of(refs, start, count):
    return jnp.concatenate([ref[start : start + count] for ref in refs], axis=0)


def rate_row(refs, rows):
    return jnp.concatenate([ref[2 * rows :, :rows].astype(F32)[:1] for ref in refs], axis=1)


def groups_of(refs):
    size = len(refs) // STEPS
    return [(step, refs[step * size : (step + 1) * size]) for step in range(STEPS)]


def start_all(pairs, sem_ref, first=0):
    copies = [
        pltpu.make_async_copy(source, target, sem_ref.at[first + number])
        for number, (source, target) in enumerate(pairs)
    ]
    for copy in copies:
        copy.start()
    return copies


def add_to(acc_ref, out_ref, step, index, value):
    owners, _, share, width = out_ref.shape
    if step:
        value = acc_ref[index] + value
    if step < STEPS - 1:
        acc_ref[index] = value
    else:
        out_ref[:, index] = value.astype(BF16).reshape(owners, share, width)


def whole(ref, index):
    part = ref[:, index]
    return part.reshape(part.shape[0] * part.shape[1], part.shape[2])


def give(refs, value, start, rows):
    rounded = value.T.astype(BF16)
    for slot, ref in enumerate(refs):
        ref[start : start + rows] = rounded[slot * rows : (slot + 1) * rows]


def put_halves(x_ref, high, low, at, value):
    x_ref[(high, *at)], x_ref[(low, *at)] = halves(value)


def by_blocks(hid, tokens, visit):
    totals = [None] * (tokens // COLUMN_BLOCK)
    for start in range(0, hid, ROW_BLOCK):
        rows = slice(start, start + ROW_BLOCK)
        for column in range(tokens // COLUMN_BLOCK):
            columns = slice(column * COLUMN_BLOCK, (column + 1) * COLUMN_BLOCK)
            found = visit((rows, columns), columns)
            totals[column] = found if totals[column] is None or found is None else totals[column] + found
    return totals


def forward_halves(p_ref, x_ref, r):
    def visit(at, columns):
        a, b, d = p_ref[(0, *at)], p_ref[(1, *at)], p_ref[(2, *at)]
        s = jax.nn.sigmoid(a)
        sa = a * s
        hid = sa * b
        if r is not None:
            hid, d = hid * r[:, columns], d * r[:, columns]
        put_halves(x_ref, 4, 5, at, hid)
        put_halves(x_ref, 2, 3, at, d * sa)
        put_halves(x_ref, 0, 1, at, d * b * (s * (1.0 + a * (1.0 - s))))

    by_blocks(p_ref.shape[1], p_ref.shape[2], visit)


def first_products(p_ref, wh_ref, wl_ref, k, v):
    for index, operand in enumerate((k, k, v)):
        p_ref[index] = mm(wh_ref[index], operand, (1, 1)) + mm(wl_ref[index], operand, (1, 1))


def inner_kernel(rows, *refs):
    sources, (wh_ref, wl_ref, out_ref, acc_ref, p_ref, x_ref) = refs[:-6], refs[-6:]
    messages = pieces(sources[: len(sources) // 2], sources[len(sources) // 2 :])
    for step, group in groups_of(messages):
        put = functools.partial(add_to, acc_ref, out_ref, step)
        k, v = rows_of(group, 0, rows), rows_of(group, rows, rows)
        first_products(p_ref, wh_ref, wl_ref, k, v)
        forward_halves(p_ref, x_ref, rate_row(group, rows))
        for index, operand in enumerate((k, k, v)):
            put(index, mm(x_ref[2 * index], operand) + mm(x_ref[2 * index + 1], operand))


def outer_kernel(rows, *refs):
    layers = (len(refs) - 8) // 3
    messages, n_ref = pieces(refs[:layers], refs[layers : 2 * layers]), refs[2 * layers]
    gifts, rest = refs[2 * layers + 1 : -7], refs[-7:]
    out_ref, acc_ref, held_ref, p_ref, x_ref, left_ref, sem_ref = rest
    gifts = pieces(gifts, gifts)
    copies = []
    hid = acc_ref.shape[1]
    parts = [whole(n_ref, index) for index in range(3)]
    for index in range(4):
        left_ref[:, index * hid : (index + 1) * hid] = parts[index // 2].T
    for (step, group), (_, back) in zip(groups_of(messages), groups_of(gifts)):
        put = functools.partial(add_to, acc_ref, out_ref, step)
        q, g = rows_of(group, 0, rows), rows_of(group, rows, rows)
        for index, operand in enumerate((q, q, g)):
            p_ref[index] = mm(parts[index], operand, (1, 1))
        forward_halves(p_ref, x_ref, None)
        stacked = x_ref[0:4].reshape(4 * hid, x_ref.shape[2])
        held = [held_ref.at[step * len(back) + slot] for slot in range(len(back))]
        give(held, mm(left_ref[...], stacked), 0, rows)
        copies += start_all(list(zip(held, back)), sem_ref, step * len(back))
        for index, operand in enumerate((q, q, g)):
            put(index, mm(x_ref[2 * index], operand) + mm(x_ref[2 * index + 1], operand))
    for copy in copies:
        copy.wait()


def second_halves(act_ref, p_ref, x_ref, r):
    def visit(at, columns):
        a, b, d = act_ref[(0, *at)], act_ref[(1, *at)], act_ref[(2, *at)]
        big_a, big_b, e = p_ref[(0, *at)], p_ref[(1, *at)], p_ref[(2, *at)]
        rate = r[:, columns]
        s = jax.nn.sigmoid(a)
        sa = a * s
        left = 1.0 - s
        ds = s * (1.0 + a * left)
        dds = s * left * (2.0 + a * (left - s))
        dh, er = d * rate, e * rate
        bds, dhds = b * ds, dh * ds
        hid = sa * b
        ddh = big_a * bds + big_b * sa
        put_halves(x_ref, 0, 1, at, dh * bds)
        put_halves(x_ref, 2, 3, at, dh * sa)
        put_halves(x_ref, 6, 4, at, er * bds + big_b * dhds + big_a * (dh * b * dds))
        put_halves(x_ref, 7, 5, at, er * sa + big_a * dhds)
        put_halves(x_ref, 8, 9, at, hid * rate)
        put_halves(x_ref, 11, 10, at, ddh * rate)
        return hid * e + ddh * d

    totals = by_blocks(p_ref.shape[1], p_ref.shape[2], visit)
    return jnp.concatenate([jnp.sum(t, axis=0, keepdims=True) for t in totals], axis=1)


def second_kernel(rows, *refs):
    layers = (len(refs) - 14) // 3
    sources = pieces(refs[:layers], refs[layers : 2 * layers])
    wh_ref, wl_ref, c_ref = refs[2 * layers : 2 * layers + 3]
    gifts, rest = refs[2 * layers + 3 : -11], refs[-11:]
    gifts = pieces(gifts, gifts)
    out_ref, acc_ref, message_ref, act_ref, held_ref, p_ref, x_ref = rest[:7]
    key_left, value_left, message_sem, held_sem = rest[7:]
    messages = [message_ref.at[slot] for slot in range(len(sources))]
    loads = start_all(list(zip(sources, messages)), message_sem)
    copies = []
    hid = acc_ref.shape[1]
    parts = [whole(c_ref, index) for index in range(3)]
    gate, up, down = [part.T for part in parts]
    high, low = [wh_ref[index].T for index in range(3)], [wl_ref[index].T for index in range(3)]
    for left_ref, items in (
        (key_left, (gate, gate, up, up, high[0], high[1], high[0], high[1], low[0], low[1])),
        (value_left, (down, down, high[2], high[2], low[2])),
    ):
        for index, item in enumerate(items):
            left_ref[:, index * hid : (index + 1) * hid] = item
    for (step, group), (_, back) in zip(groups_of(messages), groups_of(gifts)):
        put = functools.partial(add_to, acc_ref, out_ref, step)
        for load in loads[step * len(group) : (step + 1) * len(group)]:
            load.wait()
        k, v = rows_of(group, 0, rows), rows_of(group, rows, rows)
        for index, operand in enumerate((k, k, v)):
            p_ref[index] = mm(parts[index], operand, (1, 1))
        first_products(act_ref, wh_ref, wl_ref, k, v)
        d_rate = second_halves(act_ref, p_ref, x_ref, rate_row(group, rows))

        def stacked(first, last):
            return x_ref[first:last].reshape((last - first) * hid, x_ref.shape[2])

        dk = mm(key_left[:, : 8 * hid], stacked(0, 8)) + mm(key_left[:, 8 * hid :], stacked(6, 8))
        dv = mm(value_left[:, : 4 * hid], stacked(8, 12)) + mm(value_left[:, 4 * hid :], x_ref[11])
        held = [held_ref.at[step * len(back) + slot] for slot in range(len(back))]
        give(held, dk, 0, rows)
        give(held, dv, rows, rows)
        for slot, ref in enumerate(held):
            ref[2 * rows :] = padded_row(d_rate[:, slot * rows : (slot + 1) * rows], ref.shape[1])
        copies += start_all(list(zip(held, back)), held_sem, step * len(back))
        for index, (one, two, operand) in enumerate(((6, 4, k), (7, 5, k), (11, 10, v))):
            put(index, mm(x_ref[one], operand) + mm(x_ref[two], operand))
    for copy in copies:
        copy.wait()


def total_of(in_ref):
    total = in_ref[0].astype(F32)
    for source in range(1, in_ref.shape[0]):
        total += in_ref[source].astype(F32)
    return total


def norm_of(rows):
    return jnp.sqrt(jnp.sum(rows * rows, axis=-1, keepdims=True) + EPSILON)


def spread(value, out_ref):
    rounded = value.astype(BF16)
    for owner in range(out_ref.shape[0]):
        out_ref[owner] = rounded


def update_kernel(in_ref, w_ref, out_ref, moved_ref):
    w = w_ref[...]
    moved = w + total_of(in_ref)
    moved_ref[...] = moved
    spread(moved * (norm_of(w) / norm_of(moved)), out_ref)


def back_kernel(in_ref, w_ref, moved_ref, out_ref, direct_ref):
    w, moved = w_ref[...], moved_ref[...]
    given = total_of(in_ref)
    old, new = norm_of(w), norm_of(moved)
    along = jnp.sum(given * moved, axis=-1, keepdims=True) / new
    cotangent = (given - moved * (along / new)) * (old / new)
    direct_ref[...] = cotangent + w * (along / old)
    spread(cotangent, out_ref)


def last_kernel(in_ref, direct_ref, out_ref):
    out_ref[...] = total_of(in_ref) + direct_ref[...]


def body(query_tokens, key_tokens, value_tokens, step_sizes, fast_weights, out_grad):
    rows = query_tokens.shape[0]
    layers, cores = lax.axis_size("z"), lax.axis_size("c")
    heads = layers * cores
    owners = lax.axis_size("p")
    width = query_tokens.shape[1] // heads
    hid = fast_weights.shape[2]
    share = hid // owners
    layer, place, core = lax.axis_index("z"), lax.axis_index("p"), lax.axis_index("c")
    product = 2 * heads * rows * hid * width
    shifts = [0, layers // 2] + [up for up in range(1, layers) if up != layers // 2]
    places = jnp.stack(
        [(layer + up) % layers * cores + (core + over) % cores for over in range(cores) for up in shifts]
    ).astype(jnp.int32)

    def along(messages, sign):
        pairs = [[(z, (z + sign * up) % layers) for z in range(layers)] for up in shifts]
        moved = [lax.ppermute(m, "z", pair) for m, pair in zip(messages[1:], pairs[1:])]
        return [messages[0]] + moved

    def across(messages):
        return [lax.ppermute(message, "c", [(0, 1), (1, 0)]) for message in messages]

    def scatter(message):
        message = message.reshape(owners, 3 * share, width)
        return lax.all_to_all(message, "p", 0, 0, tiled=True)

    weights = lax.dynamic_index_in_dim(fast_weights, core, 0, keepdims=False)
    own = lax.dynamic_slice_in_dim(weights, place * share, share, 1).reshape(3 * share, width)
    rounded = lax.reduce_precision(weights, 8, 7)
    w_high, w_low = rounded.astype(BF16), (weights - rounded).astype(BF16)
    memory = pl.BlockSpec(memory_space=pltpu.VMEM)
    scalars = pl.BlockSpec(memory_space=pltpu.SMEM)

    def messages_of(count):
        return (shape((cores * count, width), BF16),) * layers

    kv = along(
        call(
            pack_kv_kernel, messages_of(2 * rows + PAD), in_specs=[scalars, memory, memory, memory]
        )(places, key_tokens, value_tokens, step_sizes.T),
        1,
    )
    kv += across(kv)
    qg = along(
        call(pack_qg_kernel, messages_of(2 * rows), in_specs=[scalars, memory, memory])(
            places, query_tokens, out_grad
        ),
        1,
    )
    part_shape = shape((owners, 3, share, width), BF16)
    scratch = [pltpu.VMEM((3, hid, width), F32)]
    group_tokens = heads * rows // STEPS
    products = pltpu.VMEM((3, hid, group_tokens), F32)
    half_terms = pltpu.VMEM((6, hid, group_tokens), BF16)
    main = pl.BlockSpec(memory_space=pltpu.HBM)
    grad_part = call(
        functools.partial(inner_kernel, rows),
        part_shape,
        flops=12 * product,
        vmem=60,
        in_specs=[memory] * (heads + 2),
        out_specs=memory,
        scratch_shapes=scratch + [products, half_terms],
    )(*kv, w_high, w_low)
    own_shape = shape((3 * share, width), F32)
    spread_shape = shape((owners, 3 * share, width), BF16)
    summed, qg[1] = lax.optimization_barrier((scatter(grad_part), qg[1]))
    updated, moved = call(update_kernel, (spread_shape, own_shape))(summed, own)
    updated, got = lax.optimization_barrier((scatter(updated), across(qg)))
    updated, qg = updated.reshape(owners, 3, share, width), qg + got
    *d_queries, d_part = call(
        functools.partial(outer_kernel, rows),
        messages_of(rows) + (part_shape,),
        flops=13 * product,
        vmem=60,
        in_specs=[memory] * (heads + 1),
        out_specs=[main] * layers + [memory],
        scratch_shapes=scratch
        + [
            pltpu.VMEM((heads, rows, width), BF16),
            products,
            half_terms,
            pltpu.VMEM((width, 4 * hid), BF16),
            pltpu.SemaphoreType.DMA((heads,)),
        ],
    )(*qg, updated)
    given, d_queries = lax.optimization_barrier((scatter(d_part), along(d_queries, -1)))
    cotangent, direct = call(back_kernel, (spread_shape, own_shape))(given, own, moved)
    wide = (rows, heads * width)
    taken = [scalars] + [memory] * heads
    query_grad = call(unpack_q_kernel, shape(wide, BF16), in_specs=taken)(
        places, *d_queries, *across(d_queries)
    )
    cotangent, query_grad = lax.optimization_barrier((scatter(cotangent), query_grad))
    cotangent = cotangent.reshape(owners, 3, share, width)
    *d_kv, second_part = call(
        functools.partial(second_kernel, rows),
        messages_of(2 * rows + PAD) + (part_shape,),
        flops=24 * product,
        vmem=60,
        in_specs=[main] * heads + [memory] * 3,
        out_specs=[main] * layers + [memory],
        scratch_shapes=scratch
        + [
            pltpu.VMEM((heads, 2 * rows + PAD, width), BF16),
            products,
            pltpu.VMEM((heads, 2 * rows + PAD, width), BF16),
            products,
            pltpu.VMEM((12, hid, group_tokens), BF16),
            pltpu.VMEM((width, 10 * hid), BF16),
            pltpu.VMEM((width, 5 * hid), BF16),
            pltpu.SemaphoreType.DMA((heads,)),
            pltpu.SemaphoreType.DMA((heads,)),
        ],
    )(*kv, w_high, w_low, cotangent)
    d_kv = along(d_kv, -1)
    key_grad, value_grad, step_grad = call(
        unpack_kv_kernel,
        (shape(wide, BF16), shape(wide, BF16), shape((heads, rows), BF16)),
        in_specs=taken,
    )(places, *d_kv, *across(d_kv))
    step_grad = step_grad.T
    summed = call(last_kernel, own_shape)(scatter(second_part), direct)
    summed = summed.reshape(3, 2, share // 2, width)
    kept = lax.dynamic_index_in_dim(summed, core, 1, keepdims=False)
    sent = lax.dynamic_index_in_dim(summed, 1 - core, 1, keepdims=False)
    got = lax.ppermute(sent, "c", [(0, 1), (1, 0)])
    first = core == 0
    meta_grad = jnp.stack([jnp.where(first, kept, got), jnp.where(first, got, kept)])
    return meta_grad, query_grad, key_grad, value_grad, step_grad


def solution(mesh):
    layers, lines = mesh.devices.shape
    small = Mesh(mesh.devices.reshape(layers, lines // 2, 2), ("z", "p", "c"))
    rows = P(("z", "p", "c"), None)
    return jax.shard_map(
        body,
        mesh=small,
        in_specs=(rows, rows, rows, rows, P("z", None, None, None), rows),
        out_specs=(P("z", None, ("p", "c"), None), rows, rows, rows, rows),
        check_vma=False,
    )
```

```python
import functools

import jax
import jax.numpy as jnp
from jax import lax
from jax.experimental import pallas as pl
from jax.experimental.pallas import tpu as pltpu
from jax.sharding import Mesh
from jax.sharding import PartitionSpec as P

EPSILON = 1e-05
PAD = 16
STEPS = 2
ROW_BLOCK = 16
COLUMN_BLOCK = 256
F32 = jnp.float32
BF16 = jnp.bfloat16


def mm(left, right, contract=(1, 0)):
    return lax.dot_general(
        left, right, (((contract[0],), (contract[1],)), ((), ())), preferred_element_type=F32
    )


def halves(value):
    high = value.astype(BF16)
    return high, (value - high.astype(F32)).astype(BF16)


def call(kernel, out_shape, flops=0, size=4 << 20, vmem=8, **options):
    return pl.pallas_call(
        kernel,
        out_shape=out_shape,
        compiler_params=pltpu.CompilerParams(vmem_limit_bytes=vmem << 20),
        cost_estimate=pl.CostEstimate(flops=flops, bytes_accessed=size, transcendentals=0),
        **options,
    )


def shape(dims, dtype):
    return jax.ShapeDtypeStruct(dims, dtype)


def mask_row(dims, index):
    return lax.broadcasted_iota(jnp.int32, dims, 0) == index


def padded_row(row, width):
    block = jnp.broadcast_to(row, (PAD, row.shape[1]))
    return jnp.concatenate([block] * (width // row.shape[1]), axis=1).astype(BF16)


def columns_of(place_ref, slot, width):
    return pl.ds(pl.multiple_of(place_ref[slot] * width, width), width)


def pieces(own_refs, got_refs):
    half = own_refs[0].shape[0] // 2
    return [ref.at[:half] for ref in own_refs] + [ref.at[half:] for ref in got_refs]


def pack_kv_kernel(place_ref, key_ref, value_ref, rate_ref, *out_refs):
    rows, width = key_ref.shape[0], out_refs[0].shape[1]
    rates = rate_ref[...].astype(F32)
    for slot, out_ref in enumerate(pieces(out_refs, out_refs)):
        columns = columns_of(place_ref, slot, width)
        out_ref[:rows] = key_ref[:, columns]
        out_ref[rows : 2 * rows] = value_ref[:, columns]
        chosen = jnp.where(mask_row(rates.shape, place_ref[slot]), rates, 0.0)
        out_ref[2 * rows :] = padded_row(jnp.sum(chosen, axis=0, keepdims=True), width)


def pack_qg_kernel(place_ref, query_ref, cotangent_ref, *out_refs):
    rows, width = query_ref.shape[0], out_refs[0].shape[1]
    for slot, out_ref in enumerate(pieces(out_refs, out_refs)):
        columns = columns_of(place_ref, slot, width)
        out_ref[:rows] = query_ref[:, columns]
        out_ref[rows:] = cotangent_ref[:, columns]


def unpack_kv_kernel(place_ref, *refs):
    in_refs, (key_ref, value_ref, rate_ref) = refs[:-3], refs[-3:]
    rows, width = key_ref.shape[0], in_refs[0].shape[1]
    count = len(in_refs) // 2
    rates = jnp.zeros(rate_ref.shape, F32)
    for slot, in_ref in enumerate(pieces(in_refs[:count], in_refs[count:])):
        columns = columns_of(place_ref, slot, width)
        key_ref[:, columns] = in_ref[:rows]
        value_ref[:, columns] = in_ref[rows : 2 * rows]
        row = in_ref[2 * rows :, :rows].astype(F32)[:1]
        rates = jnp.where(mask_row(rates.shape, place_ref[slot]), row, rates)
    rate_ref[...] = rates.astype(BF16)


def unpack_q_kernel(place_ref, *refs):
    in_refs, query_ref = refs[:-1], refs[-1]
    width, count = in_refs[0].shape[1], len(in_refs) // 2
    for slot, in_ref in enumerate(pieces(in_refs[:count], in_refs[count:])):
        query_ref[:, columns_of(place_ref, slot, width)] = in_ref[...]


def rows_of(refs, start, count):
    return jnp.concatenate([ref[start : start + count] for ref in refs], axis=0)


def rate_row(refs, rows):
    return jnp.concatenate([ref[2 * rows :, :rows].astype(F32)[:1] for ref in refs], axis=1)


def groups_of(refs):
    size = len(refs) // STEPS
    return [(step, refs[step * size : (step + 1) * size]) for step in range(STEPS)]


def start_all(pairs, sem_ref, first=0):
    copies = [
        pltpu.make_async_copy(source, target, sem_ref.at[first + number])
        for number, (source, target) in enumerate(pairs)
    ]
    for copy in copies:
        copy.start()
    return copies


def add_to(acc_ref, out_ref, step, index, value):
    owners, _, share, width = out_ref.shape
    if step:
        value = acc_ref[index] + value
    if step < STEPS - 1:
        acc_ref[index] = value
    else:
        out_ref[:, index] = value.astype(BF16).reshape(owners, share, width)


def whole(ref, index):
    part = ref[:, index]
    return part.reshape(part.shape[0] * part.shape[1], part.shape[2])


def give(refs, value, start, rows):
    rounded = value.astype(BF16).T
    for slot, ref in enumerate(refs):
        ref[start : start + rows] = rounded[slot * rows : (slot + 1) * rows]


def put_halves(x_ref, high, low, at, value):
    x_ref[(high, *at)], x_ref[(low, *at)] = halves(value)


def by_blocks(hid, tokens, visit):
    totals = [None] * (tokens // COLUMN_BLOCK)
    for start in range(0, hid, ROW_BLOCK):
        rows = slice(start, start + ROW_BLOCK)
        for column in range(tokens // COLUMN_BLOCK):
            columns = slice(column * COLUMN_BLOCK, (column + 1) * COLUMN_BLOCK)
            found = visit((rows, columns), columns)
            totals[column] = found if totals[column] is None or found is None else totals[column] + found
    return totals


def forward_halves(p_ref, x_ref, r):
    def visit(at, columns):
        a, b, d = p_ref[(0, *at)], p_ref[(1, *at)], p_ref[(2, *at)]
        s = jax.nn.sigmoid(a)
        sa = a * s
        hid = sa * b
        if r is not None:
            hid, d = hid * r[:, columns], d * r[:, columns]
        put_halves(x_ref, 4, 5, at, hid)
        put_halves(x_ref, 2, 3, at, d * sa)
        put_halves(x_ref, 0, 1, at, d * b * (s * (1.0 + a * (1.0 - s))))

    by_blocks(p_ref.shape[1], p_ref.shape[2], visit)


def first_products(p_ref, wh_ref, wl_ref, k, v):
    for index, operand in enumerate((k, k, v)):
        p_ref[index] = mm(wh_ref[index], operand, (1, 1)) + mm(wl_ref[index], operand, (1, 1))


def inner_kernel(rows, *refs):
    sources, rest = refs[:-7], refs[-7:]
    w_ref, out_ref, acc_ref, p_ref, x_ref, wh_ref, wl_ref = rest
    for index in range(3):
        wh_ref[index], wl_ref[index] = halves(w_ref[index])
    messages = pieces(sources[: len(sources) // 2], sources[len(sources) // 2 :])
    for step, group in groups_of(messages):
        put = functools.partial(add_to, acc_ref, out_ref, step)
        k, v = rows_of(group, 0, rows), rows_of(group, rows, rows)
        first_products(p_ref, wh_ref, wl_ref, k, v)
        forward_halves(p_ref, x_ref, rate_row(group, rows))
        for index, operand in enumerate((k, k, v)):
            put(index, mm(x_ref[2 * index], operand) + mm(x_ref[2 * index + 1], operand))


def outer_kernel(rows, *refs):
    layers = (len(refs) - 8) // 3
    messages, n_ref = pieces(refs[:layers], refs[layers : 2 * layers]), refs[2 * layers]
    gifts, rest = refs[2 * layers + 1 : -7], refs[-7:]
    out_ref, acc_ref, held_ref, p_ref, x_ref, left_ref, sem_ref = rest
    gifts = pieces(gifts, gifts)
    copies = []
    hid = acc_ref.shape[1]
    parts = [whole(n_ref, index) for index in range(3)]
    for index in range(4):
        left_ref[:, index * hid : (index + 1) * hid] = parts[index // 2].T
    for (step, group), (_, back) in zip(groups_of(messages), groups_of(gifts)):
        put = functools.partial(add_to, acc_ref, out_ref, step)
        q, g = rows_of(group, 0, rows), rows_of(group, rows, rows)
        for index, operand in enumerate((q, q, g)):
            p_ref[index] = mm(parts[index], operand, (1, 1))
        forward_halves(p_ref, x_ref, None)
        stacked = x_ref[0:4].reshape(4 * hid, x_ref.shape[2])
        held = [held_ref.at[step * len(back) + slot] for slot in range(len(back))]
        give(held, mm(left_ref[...], stacked), 0, rows)
        copies += start_all(list(zip(held, back)), sem_ref, step * len(back))
        for index, operand in enumerate((q, q, g)):
            put(index, mm(x_ref[2 * index], operand) + mm(x_ref[2 * index + 1], operand))
    for copy in copies:
        copy.wait()


def second_halves(act_ref, p_ref, x_ref, r):
    def visit(at, columns):
        a, b, d = act_ref[(0, *at)], act_ref[(1, *at)], act_ref[(2, *at)]
        big_a, big_b, e = p_ref[(0, *at)], p_ref[(1, *at)], p_ref[(2, *at)]
        rate = r[:, columns]
        s = jax.nn.sigmoid(a)
        sa = a * s
        left = 1.0 - s
        ds = s * (1.0 + a * left)
        dds = s * left * (2.0 + a * (left - s))
        dh, er = d * rate, e * rate
        bds, dhds = b * ds, dh * ds
        hid = sa * b
        ddh = big_a * bds + big_b * sa
        put_halves(x_ref, 0, 1, at, dh * bds)
        put_halves(x_ref, 2, 3, at, dh * sa)
        put_halves(x_ref, 6, 4, at, er * bds + big_b * dhds + big_a * (dh * b * dds))
        put_halves(x_ref, 7, 5, at, er * sa + big_a * dhds)
        put_halves(x_ref, 8, 9, at, hid * rate)
        put_halves(x_ref, 11, 10, at, ddh * rate)
        return hid * e + ddh * d

    totals = by_blocks(p_ref.shape[1], p_ref.shape[2], visit)
    return jnp.concatenate([jnp.sum(t, axis=0, keepdims=True) for t in totals], axis=1)


def second_kernel(rows, *refs):
    layers = (len(refs) - 14) // 3
    sources = pieces(refs[:layers], refs[layers : 2 * layers])
    wh_ref, wl_ref, c_ref = refs[2 * layers : 2 * layers + 3]
    gifts, rest = refs[2 * layers + 3 : -11], refs[-11:]
    gifts = pieces(gifts, gifts)
    out_ref, acc_ref, message_ref, act_ref, held_ref, p_ref, x_ref = rest[:7]
    key_left, value_left, message_sem, held_sem = rest[7:]
    messages = [message_ref.at[slot] for slot in range(len(sources))]
    loads = start_all(list(zip(sources, messages)), message_sem)
    copies = []
    hid = acc_ref.shape[1]
    parts = [whole(c_ref, index) for index in range(3)]
    gate, up, down = [part.T for part in parts]
    high, low = [wh_ref[index].T for index in range(3)], [wl_ref[index].T for index in range(3)]
    for left_ref, items in (
        (key_left, (gate, gate, up, up, high[0], high[1], high[0], high[1], low[0], low[1])),
        (value_left, (down, down, high[2], high[2], low[2])),
    ):
        for index, item in enumerate(items):
            left_ref[:, index * hid : (index + 1) * hid] = item
    for (step, group), (_, back) in zip(groups_of(messages), groups_of(gifts)):
        put = functools.partial(add_to, acc_ref, out_ref, step)
        for load in loads[step * len(group) : (step + 1) * len(group)]:
            load.wait()
        k, v = rows_of(group, 0, rows), rows_of(group, rows, rows)
        for index, operand in enumerate((k, k, v)):
            p_ref[index] = mm(parts[index], operand, (1, 1))
        first_products(act_ref, wh_ref, wl_ref, k, v)
        d_rate = second_halves(act_ref, p_ref, x_ref, rate_row(group, rows))

        def stacked(first, last):
            return x_ref[first:last].reshape((last - first) * hid, x_ref.shape[2])

        dk = mm(key_left[:, : 8 * hid], stacked(0, 8)) + mm(key_left[:, 8 * hid :], stacked(6, 8))
        dv = mm(value_left[:, : 4 * hid], stacked(8, 12)) + mm(value_left[:, 4 * hid :], x_ref[11])
        held = [held_ref.at[step * len(back) + slot] for slot in range(len(back))]
        give(held, dk, 0, rows)
        give(held, dv, rows, rows)
        for slot, ref in enumerate(held):
            ref[2 * rows :] = padded_row(d_rate[:, slot * rows : (slot + 1) * rows], ref.shape[1])
        copies += start_all(list(zip(held, back)), held_sem, step * len(back))
        for index, (one, two, operand) in enumerate(((6, 4, k), (7, 5, k), (11, 10, v))):
            put(index, mm(x_ref[one], operand) + mm(x_ref[two], operand))
    for copy in copies:
        copy.wait()


def total_of(in_ref):
    total = in_ref[0].astype(F32)
    for source in range(1, in_ref.shape[0]):
        total += in_ref[source].astype(F32)
    return total


def norm_of(rows):
    return jnp.sqrt(jnp.sum(rows * rows, axis=-1, keepdims=True) + EPSILON)


def spread(value, out_ref):
    rounded = value.astype(BF16)
    for owner in range(out_ref.shape[0]):
        out_ref[owner] = rounded


def update_kernel(in_ref, w_ref, out_ref, moved_ref):
    w = w_ref[...]
    moved = w + total_of(in_ref)
    moved_ref[...] = moved
    spread(moved * (norm_of(w) / norm_of(moved)), out_ref)


def back_kernel(in_ref, w_ref, moved_ref, out_ref, direct_ref):
    w, moved = w_ref[...], moved_ref[...]
    given = total_of(in_ref)
    old, new = norm_of(w), norm_of(moved)
    along = jnp.sum(given * moved, axis=-1, keepdims=True) / new
    cotangent = (given - moved * (along / new)) * (old / new)
    direct_ref[...] = cotangent + w * (along / old)
    spread(cotangent, out_ref)


def last_kernel(in_ref, direct_ref, out_ref):
    out_ref[...] = total_of(in_ref) + direct_ref[...]


def body(query_tokens, key_tokens, value_tokens, step_sizes, fast_weights, out_grad):
    rows = query_tokens.shape[0]
    layers, cores = lax.axis_size("z"), lax.axis_size("c")
    heads = layers * cores
    owners = lax.axis_size("p")
    width = query_tokens.shape[1] // heads
    hid = fast_weights.shape[2]
    share = hid // owners
    layer, place, core = lax.axis_index("z"), lax.axis_index("p"), lax.axis_index("c")
    product = 2 * heads * rows * hid * width
    shifts = [0, layers // 2] + [up for up in range(1, layers) if up != layers // 2]
    places = jnp.stack(
        [(layer + up) % layers * cores + (core + over) % cores for over in range(cores) for up in shifts]
    ).astype(jnp.int32)

    def along(messages, sign):
        pairs = [[(z, (z + sign * up) % layers) for z in range(layers)] for up in shifts]
        moved = [lax.ppermute(m, "z", pair) for m, pair in zip(messages[1:], pairs[1:])]
        return [messages[0]] + moved

    def across(messages):
        return [lax.ppermute(message, "c", [(0, 1), (1, 0)]) for message in messages]

    def scatter(message):
        message = message.reshape(owners, 3 * share, width)
        return lax.all_to_all(message, "p", 0, 0, tiled=True)

    weights = lax.dynamic_index_in_dim(fast_weights, core, 0, keepdims=False)
    own = lax.dynamic_slice_in_dim(weights, place * share, share, 1).reshape(3 * share, width)
    rounded = lax.reduce_precision(weights, 8, 7)
    w_high, w_low = rounded.astype(BF16), (weights - rounded).astype(BF16)
    memory = pl.BlockSpec(memory_space=pltpu.VMEM)
    scalars = pl.BlockSpec(memory_space=pltpu.SMEM)

    def messages_of(count):
        return (shape((cores * count, width), BF16),) * layers

    kv = along(
        call(
            pack_kv_kernel, messages_of(2 * rows + PAD), in_specs=[scalars, memory, memory, memory]
        )(places, key_tokens, value_tokens, step_sizes.T),
        1,
    )
    kv += across(kv)
    qg = along(
        call(pack_qg_kernel, messages_of(2 * rows), in_specs=[scalars, memory, memory])(
            places, query_tokens, out_grad
        ),
        1,
    )
    part_shape = shape((owners, 3, share, width), BF16)
    scratch = [pltpu.VMEM((3, hid, width), F32)]
    group_tokens = heads * rows // STEPS
    products = pltpu.VMEM((3, hid, group_tokens), F32)
    half_terms = pltpu.VMEM((6, hid, group_tokens), BF16)
    main = pl.BlockSpec(memory_space=pltpu.HBM)
    grad_part = call(
        functools.partial(inner_kernel, rows),
        part_shape,
        flops=12 * product,
        vmem=60,
        in_specs=[memory] * (heads + 1),
        out_specs=memory,
        scratch_shapes=scratch + [products, half_terms] + [pltpu.VMEM((3, hid, width), BF16)] * 2,
    )(*kv, weights)
    own_shape = shape((3 * share, width), F32)
    spread_shape = shape((owners, 3 * share, width), BF16)
    summed, qg[1] = lax.optimization_barrier((scatter(grad_part), qg[1]))
    updated, moved = call(update_kernel, (spread_shape, own_shape))(summed, own)
    updated, got = lax.optimization_barrier((scatter(updated), across(qg)))
    updated, qg = updated.reshape(owners, 3, share, width), qg + got
    *d_queries, d_part = call(
        functools.partial(outer_kernel, rows),
        messages_of(rows) + (part_shape,),
        flops=13 * product,
        vmem=60,
        in_specs=[memory] * (heads + 1),
        out_specs=[main] * layers + [memory],
        scratch_shapes=scratch
        + [
            pltpu.VMEM((heads, rows, width), BF16),
            products,
            half_terms,
            pltpu.VMEM((width, 4 * hid), BF16),
            pltpu.SemaphoreType.DMA((heads,)),
        ],
    )(*qg, updated)
    given, d_queries = lax.optimization_barrier((scatter(d_part), along(d_queries, -1)))
    cotangent, direct = call(back_kernel, (spread_shape, own_shape))(given, own, moved)
    wide = (rows, heads * width)
    taken = [scalars] + [memory] * heads
    query_grad = call(unpack_q_kernel, shape(wide, BF16), in_specs=taken)(
        places, *d_queries, *across(d_queries)
    )
    cotangent, query_grad = lax.optimization_barrier((scatter(cotangent), query_grad))
    cotangent = cotangent.reshape(owners, 3, share, width)
    *d_kv, second_part = call(
        functools.partial(second_kernel, rows),
        messages_of(2 * rows + PAD) + (part_shape,),
        flops=24 * product,
        vmem=60,
        in_specs=[main] * heads + [memory] * 3,
        out_specs=[main] * layers + [memory],
        scratch_shapes=scratch
        + [
            pltpu.VMEM((heads, 2 * rows + PAD, width), BF16),
            products,
            pltpu.VMEM((heads, 2 * rows + PAD, width), BF16),
            products,
            pltpu.VMEM((12, hid, group_tokens), BF16),
            pltpu.VMEM((width, 10 * hid), BF16),
            pltpu.VMEM((width, 5 * hid), BF16),
            pltpu.SemaphoreType.DMA((heads,)),
            pltpu.SemaphoreType.DMA((heads,)),
        ],
    )(*kv, w_high, w_low, cotangent)
    d_kv = along(d_kv, -1)
    summed = call(last_kernel, own_shape)(scatter(second_part), direct)
    summed = summed.reshape(3, 2, share // 2, width)
    kept = lax.dynamic_index_in_dim(summed, core, 1, keepdims=False)
    sent = lax.dynamic_index_in_dim(summed, 1 - core, 1, keepdims=False)
    got = lax.ppermute(sent, "c", [(0, 1), (1, 0)])
    first = core == 0
    meta_grad = jnp.stack([jnp.where(first, kept, got), jnp.where(first, got, kept)])
    got, meta_grad = lax.optimization_barrier((across(d_kv), meta_grad))
    key_grad, value_grad, step_grad = call(
        unpack_kv_kernel,
        (shape(wide, BF16), shape(wide, BF16), shape((heads, rows), BF16)),
        in_specs=taken,
    )(places, *d_kv, *got)
    step_grad = step_grad.T
    return meta_grad, query_grad, key_grad, value_grad, step_grad


def solution(mesh):
    layers, lines = mesh.devices.shape
    small = Mesh(mesh.devices.reshape(layers, lines // 2, 2), ("z", "p", "c"))
    rows = P(("z", "p", "c"), None)
    return jax.shard_map(
        body,
        mesh=small,
        in_specs=(rows, rows, rows, rows, P("z", None, None, None), rows),
        out_specs=(P("z", None, ("p", "c"), None), rows, rows, rows, rows),
        check_vma=False,
    )
```

```python
import functools

import jax
import jax.numpy as jnp
from jax import lax
from jax.experimental import pallas as pl
from jax.experimental.pallas import tpu as pltpu
from jax.sharding import Mesh
from jax.sharding import PartitionSpec as P

EPSILON = 1e-05
PAD = 16
STEPS = 2
ROW_BLOCK = 16
COLUMN_BLOCK = 256
F32 = jnp.float32
BF16 = jnp.bfloat16


def mm(left, right, contract=(1, 0)):
    return lax.dot_general(
        left, right, (((contract[0],), (contract[1],)), ((), ())), preferred_element_type=F32
    )


def halves(value):
    high = value.astype(BF16)
    return high, (value - high.astype(F32)).astype(BF16)


def call(kernel, out_shape, flops=0, size=4 << 20, vmem=8, **options):
    return pl.pallas_call(
        kernel,
        out_shape=out_shape,
        compiler_params=pltpu.CompilerParams(vmem_limit_bytes=vmem << 20),
        cost_estimate=pl.CostEstimate(flops=flops, bytes_accessed=size, transcendentals=0),
        **options,
    )


def shape(dims, dtype):
    return jax.ShapeDtypeStruct(dims, dtype)


def mask_row(dims, index):
    return lax.broadcasted_iota(jnp.int32, dims, 0) == index


def padded_row(row, width):
    block = jnp.broadcast_to(row, (PAD, row.shape[1]))
    return jnp.concatenate([block] * (width // row.shape[1]), axis=1).astype(BF16)


def columns_of(place_ref, slot, width):
    return pl.ds(pl.multiple_of(place_ref[slot] * width, width), width)


def pieces(own_refs, got_refs):
    half = own_refs[0].shape[0] // 2
    return [ref.at[:half] for ref in own_refs] + [ref.at[half:] for ref in got_refs]


def pack_kv_kernel(place_ref, key_ref, value_ref, rate_ref, *out_refs):
    rows, width = key_ref.shape[0], out_refs[0].shape[1]
    rates = rate_ref[...].astype(F32)
    for slot, out_ref in enumerate(pieces(out_refs, out_refs)):
        columns = columns_of(place_ref, slot, width)
        out_ref[:rows] = key_ref[:, columns]
        out_ref[rows : 2 * rows] = value_ref[:, columns]
        chosen = jnp.where(mask_row(rates.shape, place_ref[slot]), rates, 0.0)
        out_ref[2 * rows :] = padded_row(jnp.sum(chosen, axis=0, keepdims=True), width)


def pack_qg_kernel(place_ref, query_ref, cotangent_ref, *out_refs):
    rows, width = query_ref.shape[0], out_refs[0].shape[1]
    for slot, out_ref in enumerate(pieces(out_refs, out_refs)):
        columns = columns_of(place_ref, slot, width)
        out_ref[:rows] = query_ref[:, columns]
        out_ref[rows:] = cotangent_ref[:, columns]


def unpack_kv_kernel(place_ref, *refs):
    in_refs, (key_ref, value_ref, rate_ref) = refs[:-3], refs[-3:]
    rows, width = key_ref.shape[0], in_refs[0].shape[1]
    count = len(in_refs) // 2
    rates = jnp.zeros(rate_ref.shape, F32)
    for slot, in_ref in enumerate(pieces(in_refs[:count], in_refs[count:])):
        columns = columns_of(place_ref, slot, width)
        key_ref[:, columns] = in_ref[:rows]
        value_ref[:, columns] = in_ref[rows : 2 * rows]
        row = in_ref[2 * rows :, :rows].astype(F32)[:1]
        rates = jnp.where(mask_row(rates.shape, place_ref[slot]), row, rates)
    rate_ref[...] = rates.astype(BF16)


def unpack_q_kernel(place_ref, *refs):
    in_refs, query_ref = refs[:-1], refs[-1]
    width, count = in_refs[0].shape[1], len(in_refs) // 2
    for slot, in_ref in enumerate(pieces(in_refs[:count], in_refs[count:])):
        query_ref[:, columns_of(place_ref, slot, width)] = in_ref[...]


def rows_of(refs, start, count):
    return jnp.concatenate([ref[start : start + count] for ref in refs], axis=0)


def rate_row(refs, rows):
    return jnp.concatenate([ref[2 * rows :, :rows].astype(F32)[:1] for ref in refs], axis=1)


def groups_of(refs):
    size = len(refs) // STEPS
    return [(step, refs[step * size : (step + 1) * size]) for step in range(STEPS)]


def add_to(acc_ref, out_ref, step, index, value):
    owners, _, share, width = out_ref.shape
    if step:
        value = acc_ref[index] + value
    if step < STEPS - 1:
        acc_ref[index] = value
    else:
        out_ref[:, index] = value.astype(BF16).reshape(owners, share, width)


def whole(ref, index):
    part = ref[:, index]
    return part.reshape(part.shape[0] * part.shape[1], part.shape[2])


def give(refs, value, start, rows):
    rounded = value.astype(BF16).T
    for slot, ref in enumerate(refs):
        ref[start : start + rows] = rounded[slot * rows : (slot + 1) * rows]


def put_halves(x_ref, high, low, at, value):
    x_ref[(high, *at)], x_ref[(low, *at)] = halves(value)


def by_blocks(hid, tokens, visit):
    totals = [None] * (tokens // COLUMN_BLOCK)
    for start in range(0, hid, ROW_BLOCK):
        rows = slice(start, start + ROW_BLOCK)
        for column in range(tokens // COLUMN_BLOCK):
            columns = slice(column * COLUMN_BLOCK, (column + 1) * COLUMN_BLOCK)
            found = visit((rows, columns), columns)
            totals[column] = found if totals[column] is None or found is None else totals[column] + found
    return totals


def forward_halves(p_ref, x_ref, r):
    def visit(at, columns):
        a, b, d = p_ref[(0, *at)], p_ref[(1, *at)], p_ref[(2, *at)]
        s = jax.nn.sigmoid(a)
        sa = a * s
        hid = sa * b
        if r is not None:
            hid, d = hid * r[:, columns], d * r[:, columns]
        put_halves(x_ref, 4, 5, at, hid)
        put_halves(x_ref, 2, 3, at, d * sa)
        put_halves(x_ref, 0, 1, at, d * b * (s * (1.0 + a * (1.0 - s))))

    by_blocks(p_ref.shape[1], p_ref.shape[2], visit)


def first_products(p_ref, wh_ref, wl_ref, k, v):
    for index, operand in enumerate((k, k, v)):
        p_ref[index] = mm(wh_ref[index], operand, (1, 1)) + mm(wl_ref[index], operand, (1, 1))


def inner_kernel(rows, *refs):
    sources, rest = refs[:-7], refs[-7:]
    w_ref, out_ref, acc_ref, p_ref, x_ref, wh_ref, wl_ref = rest
    for index in range(3):
        wh_ref[index], wl_ref[index] = halves(w_ref[index])
    messages = pieces(sources[: len(sources) // 2], sources[len(sources) // 2 :])
    for step, group in groups_of(messages):
        put = functools.partial(add_to, acc_ref, out_ref, step)
        k, v = rows_of(group, 0, rows), rows_of(group, rows, rows)
        first_products(p_ref, wh_ref, wl_ref, k, v)
        forward_halves(p_ref, x_ref, rate_row(group, rows))
        for index, operand in enumerate((k, k, v)):
            put(index, mm(x_ref[2 * index], operand) + mm(x_ref[2 * index + 1], operand))


def outer_kernel(rows, *refs):
    layers = (len(refs) - 6) // 3
    messages, n_ref = pieces(refs[:layers], refs[layers : 2 * layers]), refs[2 * layers]
    gifts, rest = refs[2 * layers + 1 : -5], refs[-5:]
    out_ref, acc_ref, p_ref, x_ref, left_ref = rest
    gifts = pieces(gifts, gifts)
    hid = acc_ref.shape[1]
    parts = [whole(n_ref, index) for index in range(3)]
    for index in range(4):
        left_ref[:, index * hid : (index + 1) * hid] = parts[index // 2].T
    for (step, group), (_, back) in zip(groups_of(messages), groups_of(gifts)):
        put = functools.partial(add_to, acc_ref, out_ref, step)
        q, g = rows_of(group, 0, rows), rows_of(group, rows, rows)
        for index, operand in enumerate((q, q, g)):
            p_ref[index] = mm(parts[index], operand, (1, 1))
        forward_halves(p_ref, x_ref, None)
        stacked = x_ref[0:4].reshape(4 * hid, x_ref.shape[2])
        held = back
        give(held, mm(left_ref[...], stacked), 0, rows)
        for index, operand in enumerate((q, q, g)):
            put(index, mm(x_ref[2 * index], operand) + mm(x_ref[2 * index + 1], operand))


def second_halves(act_ref, p_ref, x_ref, r):
    def visit(at, columns):
        a, b, d = act_ref[(0, *at)], act_ref[(1, *at)], act_ref[(2, *at)]
        big_a, big_b, e = p_ref[(0, *at)], p_ref[(1, *at)], p_ref[(2, *at)]
        rate = r[:, columns]
        s = jax.nn.sigmoid(a)
        sa = a * s
        left = 1.0 - s
        ds = s * (1.0 + a * left)
        dds = s * left * (2.0 + a * (left - s))
        dh, er = d * rate, e * rate
        bds, dhds = b * ds, dh * ds
        hid = sa * b
        ddh = big_a * bds + big_b * sa
        put_halves(x_ref, 0, 1, at, dh * bds)
        put_halves(x_ref, 2, 3, at, dh * sa)
        put_halves(x_ref, 6, 4, at, er * bds + big_b * dhds + big_a * (dh * b * dds))
        put_halves(x_ref, 7, 5, at, er * sa + big_a * dhds)
        put_halves(x_ref, 8, 9, at, hid * rate)
        put_halves(x_ref, 11, 10, at, ddh * rate)
        return hid * e + ddh * d

    totals = by_blocks(p_ref.shape[1], p_ref.shape[2], visit)
    return jnp.concatenate([jnp.sum(t, axis=0, keepdims=True) for t in totals], axis=1)


def second_kernel(rows, *refs):
    layers = (len(refs) - 10) // 3
    sources = pieces(refs[:layers], refs[layers : 2 * layers])
    wh_ref, wl_ref, c_ref = refs[2 * layers : 2 * layers + 3]
    gifts, rest = refs[2 * layers + 3 : -7], refs[-7:]
    gifts = pieces(gifts, gifts)
    out_ref, acc_ref, act_ref, p_ref, x_ref = rest[:5]
    key_left, value_left = rest[5:]
    messages = sources
    hid = acc_ref.shape[1]
    parts = [whole(c_ref, index) for index in range(3)]
    gate, up, down = [part.T for part in parts]
    high, low = [wh_ref[index].T for index in range(3)], [wl_ref[index].T for index in range(3)]
    for left_ref, items in (
        (key_left, (gate, gate, up, up, high[0], high[1], high[0], high[1], low[0], low[1])),
        (value_left, (down, down, high[2], high[2], low[2])),
    ):
        for index, item in enumerate(items):
            left_ref[:, index * hid : (index + 1) * hid] = item
    for (step, group), (_, back) in zip(groups_of(messages), groups_of(gifts)):
        put = functools.partial(add_to, acc_ref, out_ref, step)
        k, v = rows_of(group, 0, rows), rows_of(group, rows, rows)
        for index, operand in enumerate((k, k, v)):
            p_ref[index] = mm(parts[index], operand, (1, 1))
        first_products(act_ref, wh_ref, wl_ref, k, v)
        d_rate = second_halves(act_ref, p_ref, x_ref, rate_row(group, rows))

        def stacked(first, last):
            return x_ref[first:last].reshape((last - first) * hid, x_ref.shape[2])

        dk = mm(key_left[:, : 8 * hid], stacked(0, 8)) + mm(key_left[:, 8 * hid :], stacked(6, 8))
        dv = mm(value_left[:, : 4 * hid], stacked(8, 12)) + mm(value_left[:, 4 * hid :], x_ref[11])
        held = back
        give(held, dk, 0, rows)
        give(held, dv, rows, rows)
        for slot, ref in enumerate(held):
            ref[2 * rows :] = padded_row(d_rate[:, slot * rows : (slot + 1) * rows], ref.shape[1])
        for index, (one, two, operand) in enumerate(((6, 4, k), (7, 5, k), (11, 10, v))):
            put(index, mm(x_ref[one], operand) + mm(x_ref[two], operand))


def total_of(in_ref):
    total = in_ref[0].astype(F32)
    for source in range(1, in_ref.shape[0]):
        total += in_ref[source].astype(F32)
    return total


def norm_of(rows):
    return jnp.sqrt(jnp.sum(rows * rows, axis=-1, keepdims=True) + EPSILON)


def spread(value, out_ref):
    rounded = value.astype(BF16)
    for owner in range(out_ref.shape[0]):
        out_ref[owner] = rounded


def update_kernel(in_ref, w_ref, out_ref, moved_ref):
    w = w_ref[...]
    moved = w + total_of(in_ref)
    moved_ref[...] = moved
    spread(moved * (norm_of(w) / norm_of(moved)), out_ref)


def back_kernel(in_ref, w_ref, moved_ref, out_ref, direct_ref):
    w, moved = w_ref[...], moved_ref[...]
    given = total_of(in_ref)
    old, new = norm_of(w), norm_of(moved)
    along = jnp.sum(given * moved, axis=-1, keepdims=True) / new
    cotangent = (given - moved * (along / new)) * (old / new)
    direct_ref[...] = cotangent + w * (along / old)
    spread(cotangent, out_ref)


def last_kernel(in_ref, direct_ref, out_ref):
    out_ref[...] = total_of(in_ref) + direct_ref[...]


def body(query_tokens, key_tokens, value_tokens, step_sizes, fast_weights, out_grad):
    rows = query_tokens.shape[0]
    layers, cores = lax.axis_size("z"), lax.axis_size("c")
    heads = layers * cores
    owners = lax.axis_size("p")
    width = query_tokens.shape[1] // heads
    hid = fast_weights.shape[2]
    share = hid // owners
    layer, place, core = lax.axis_index("z"), lax.axis_index("p"), lax.axis_index("c")
    product = 2 * heads * rows * hid * width
    shifts = [0, layers // 2] + [up for up in range(1, layers) if up != layers // 2]
    places = jnp.stack(
        [(layer + up) % layers * cores + (core + over) % cores for over in range(cores) for up in shifts]
    ).astype(jnp.int32)

    def along(messages, sign):
        pairs = [[(z, (z + sign * up) % layers) for z in range(layers)] for up in shifts]
        moved = [lax.ppermute(m, "z", pair) for m, pair in zip(messages[1:], pairs[1:])]
        return [messages[0]] + moved

    def across(messages):
        return [lax.ppermute(message, "c", [(0, 1), (1, 0)]) for message in messages]

    def scatter(message):
        message = message.reshape(owners, 3 * share, width)
        return lax.all_to_all(message, "p", 0, 0, tiled=True)

    weights = lax.dynamic_index_in_dim(fast_weights, core, 0, keepdims=False)
    own = lax.dynamic_slice_in_dim(weights, place * share, share, 1).reshape(3 * share, width)
    rounded = lax.reduce_precision(weights, 8, 7)
    w_high, w_low = rounded.astype(BF16), (weights - rounded).astype(BF16)
    memory = pl.BlockSpec(memory_space=pltpu.VMEM)
    scalars = pl.BlockSpec(memory_space=pltpu.SMEM)

    def messages_of(count):
        return (shape((cores * count, width), BF16),) * layers

    kv = along(
        call(
            pack_kv_kernel, messages_of(2 * rows + PAD), in_specs=[scalars, memory, memory, memory]
        )(places, key_tokens, value_tokens, step_sizes.T),
        1,
    )
    kv += across(kv)
    qg = along(
        call(pack_qg_kernel, messages_of(2 * rows), in_specs=[scalars, memory, memory])(
            places, query_tokens, out_grad
        ),
        1,
    )
    part_shape = shape((owners, 3, share, width), BF16)
    scratch = [pltpu.VMEM((3, hid, width), F32)]
    group_tokens = heads * rows // STEPS
    products = pltpu.VMEM((3, hid, group_tokens), F32)
    half_terms = pltpu.VMEM((6, hid, group_tokens), BF16)
    grad_part = call(
        functools.partial(inner_kernel, rows),
        part_shape,
        flops=12 * product,
        vmem=60,
        in_specs=[memory] * (heads + 1),
        out_specs=memory,
        scratch_shapes=scratch + [products, half_terms] + [pltpu.VMEM((3, hid, width), BF16)] * 2,
    )(*kv, weights)
    own_shape = shape((3 * share, width), F32)
    spread_shape = shape((owners, 3 * share, width), BF16)
    summed, qg[1] = lax.optimization_barrier((scatter(grad_part), qg[1]))
    updated, moved = call(update_kernel, (spread_shape, own_shape))(summed, own)
    updated, got = lax.optimization_barrier((scatter(updated), across(qg)))
    updated, qg = updated.reshape(owners, 3, share, width), qg + got
    *d_queries, d_part = call(
        functools.partial(outer_kernel, rows),
        messages_of(rows) + (part_shape,),
        flops=13 * product,
        vmem=60,
        in_specs=[memory] * (heads + 1),
        out_specs=[memory] * (layers + 1),
        scratch_shapes=scratch
        + [
            products,
            half_terms,
            pltpu.VMEM((width, 4 * hid), BF16),
        ],
    )(*qg, updated)
    given, d_queries = lax.optimization_barrier((scatter(d_part), along(d_queries, -1)))
    cotangent, direct = call(back_kernel, (spread_shape, own_shape))(given, own, moved)
    wide = (rows, heads * width)
    taken = [scalars] + [memory] * heads
    query_grad = call(unpack_q_kernel, shape(wide, BF16), in_specs=taken)(
        places, *d_queries, *across(d_queries)
    )
    cotangent, query_grad = lax.optimization_barrier((scatter(cotangent), query_grad))
    cotangent = cotangent.reshape(owners, 3, share, width)
    *d_kv, second_part = call(
        functools.partial(second_kernel, rows),
        messages_of(2 * rows + PAD) + (part_shape,),
        flops=24 * product,
        vmem=60,
        in_specs=[memory] * (heads + 3),
        out_specs=[memory] * (layers + 1),
        scratch_shapes=scratch
        + [
            products,
            products,
            pltpu.VMEM((12, hid, group_tokens), BF16),
            pltpu.VMEM((width, 10 * hid), BF16),
            pltpu.VMEM((width, 5 * hid), BF16),
        ],
    )(*kv, w_high, w_low, cotangent)
    d_kv = along(d_kv, -1)
    summed = call(last_kernel, own_shape)(scatter(second_part), direct)
    summed = summed.reshape(3, 2, share // 2, width)
    kept = lax.dynamic_index_in_dim(summed, core, 1, keepdims=False)
    sent = lax.dynamic_index_in_dim(summed, 1 - core, 1, keepdims=False)
    got = lax.ppermute(sent, "c", [(0, 1), (1, 0)])
    first = core == 0
    meta_grad = jnp.stack([jnp.where(first, kept, got), jnp.where(first, got, kept)])
    got, meta_grad = lax.optimization_barrier((across(d_kv), meta_grad))
    key_grad, value_grad, step_grad = call(
        unpack_kv_kernel,
        (shape(wide, BF16), shape(wide, BF16), shape((heads, rows), BF16)),
        in_specs=taken,
    )(places, *d_kv, *got)
    step_grad = step_grad.T
    return meta_grad, query_grad, key_grad, value_grad, step_grad


def solution(mesh):
    layers, lines = mesh.devices.shape
    small = Mesh(mesh.devices.reshape(layers, lines // 2, 2), ("z", "p", "c"))
    rows = P(("z", "p", "c"), None)
    return jax.shard_map(
        body,
        mesh=small,
        in_specs=(rows, rows, rows, rows, P("z", None, None, None), rows),
        out_specs=(P("z", None, ("p", "c"), None), rows, rows, rows, rows),
        check_vma=False,
    )
```

```python
import functools

import jax
import jax.numpy as jnp
from jax import lax
from jax.experimental import pallas as pl
from jax.experimental.pallas import tpu as pltpu
from jax.sharding import Mesh
from jax.sharding import PartitionSpec as P

EPSILON = 1e-05
PAD = 16
STEPS = 2
ROW_BLOCK = 16
COLUMN_BLOCK = 512
F32 = jnp.float32
BF16 = jnp.bfloat16


def mm(left, right, contract=(1, 0)):
    return lax.dot_general(
        left, right, (((contract[0],), (contract[1],)), ((), ())), preferred_element_type=F32
    )


def halves(value):
    high = value.astype(BF16)
    return high, (value - high.astype(F32)).astype(BF16)


def call(kernel, out_shape, flops=0, size=4 << 20, vmem=8, **options):
    return pl.pallas_call(
        kernel,
        out_shape=out_shape,
        compiler_params=pltpu.CompilerParams(vmem_limit_bytes=vmem << 20),
        cost_estimate=pl.CostEstimate(flops=flops, bytes_accessed=size, transcendentals=0),
        **options,
    )


def shape(dims, dtype):
    return jax.ShapeDtypeStruct(dims, dtype)


def mask_row(dims, index):
    return lax.broadcasted_iota(jnp.int32, dims, 0) == index


def padded_row(row, width):
    block = jnp.broadcast_to(row, (PAD, row.shape[1]))
    return jnp.concatenate([block] * (width // row.shape[1]), axis=1).astype(BF16)


def columns_of(place_ref, slot, width):
    return pl.ds(pl.multiple_of(place_ref[slot] * width, width), width)


def pieces(own_refs, got_refs):
    half = own_refs[0].shape[0] // 2
    return [ref.at[:half] for ref in own_refs] + [ref.at[half:] for ref in got_refs]


def pack_kv_kernel(place_ref, key_ref, value_ref, rate_ref, *out_refs):
    rows, width = key_ref.shape[0], out_refs[0].shape[1]
    rates = rate_ref[...].astype(F32)
    for slot, out_ref in enumerate(pieces(out_refs, out_refs)):
        columns = columns_of(place_ref, slot, width)
        out_ref[:rows] = key_ref[:, columns]
        out_ref[rows : 2 * rows] = value_ref[:, columns]
        chosen = jnp.where(mask_row(rates.shape, place_ref[slot]), rates, 0.0)
        out_ref[2 * rows :] = padded_row(jnp.sum(chosen, axis=0, keepdims=True), width)


def pack_qg_kernel(place_ref, query_ref, cotangent_ref, *out_refs):
    rows, width = query_ref.shape[0], out_refs[0].shape[1]
    for slot, out_ref in enumerate(pieces(out_refs, out_refs)):
        columns = columns_of(place_ref, slot, width)
        out_ref[:rows] = query_ref[:, columns]
        out_ref[rows:] = cotangent_ref[:, columns]


def unpack_kv_kernel(place_ref, *refs):
    in_refs, (key_ref, value_ref, rate_ref) = refs[:-3], refs[-3:]
    rows, width = key_ref.shape[0], in_refs[0].shape[1]
    count = len(in_refs) // 2
    rates = jnp.zeros(rate_ref.shape, F32)
    for slot, in_ref in enumerate(pieces(in_refs[:count], in_refs[count:])):
        columns = columns_of(place_ref, slot, width)
        key_ref[:, columns] = in_ref[:rows]
        value_ref[:, columns] = in_ref[rows : 2 * rows]
        row = in_ref[2 * rows :, :rows].astype(F32)[:1]
        rates = jnp.where(mask_row(rates.shape, place_ref[slot]), row, rates)
    rate_ref[...] = rates.astype(BF16)


def unpack_q_kernel(place_ref, *refs):
    in_refs, query_ref = refs[:-1], refs[-1]
    width, count = in_refs[0].shape[1], len(in_refs) // 2
    for slot, in_ref in enumerate(pieces(in_refs[:count], in_refs[count:])):
        query_ref[:, columns_of(place_ref, slot, width)] = in_ref[...]


def rows_of(refs, start, count):
    return jnp.concatenate([ref[start : start + count] for ref in refs], axis=0)


def rate_row(refs, rows):
    return jnp.concatenate([ref[2 * rows :, :rows].astype(F32)[:1] for ref in refs], axis=1)


def groups_of(refs):
    size = len(refs) // STEPS
    return [(step, refs[step * size : (step + 1) * size]) for step in range(STEPS)]


def add_to(acc_ref, out_ref, step, index, value):
    owners, _, share, width = out_ref.shape
    if step:
        value = acc_ref[index] + value
    if step < STEPS - 1:
        acc_ref[index] = value
    else:
        out_ref[:, index] = value.astype(BF16).reshape(owners, share, width)


def whole(ref, index):
    part = ref[:, index]
    return part.reshape(part.shape[0] * part.shape[1], part.shape[2])


def give(refs, value, start, rows):
    rounded = value.astype(BF16).T
    for slot, ref in enumerate(refs):
        ref[start : start + rows] = rounded[slot * rows : (slot + 1) * rows]


def put_halves(x_ref, high, low, at, value):
    x_ref[(high, *at)], x_ref[(low, *at)] = halves(value)


def by_blocks(hid, tokens, visit):
    totals = [None] * (tokens // COLUMN_BLOCK)
    for start in range(0, hid, ROW_BLOCK):
        rows = slice(start, start + ROW_BLOCK)
        for column in range(tokens // COLUMN_BLOCK):
            columns = slice(column * COLUMN_BLOCK, (column + 1) * COLUMN_BLOCK)
            found = visit((rows, columns), columns)
            totals[column] = found if totals[column] is None or found is None else totals[column] + found
    return totals


def forward_halves(p_ref, x_ref, r):
    def visit(at, columns):
        a, b, d = p_ref[(0, *at)], p_ref[(1, *at)], p_ref[(2, *at)]
        s = jax.nn.sigmoid(a)
        sa = a * s
        hid = sa * b
        if r is not None:
            hid, d = hid * r[:, columns], d * r[:, columns]
        put_halves(x_ref, 4, 5, at, hid)
        put_halves(x_ref, 2, 3, at, d * sa)
        put_halves(x_ref, 0, 1, at, d * b * (s * (1.0 + a * (1.0 - s))))

    by_blocks(p_ref.shape[1], p_ref.shape[2], visit)


def first_products(p_ref, wh_ref, wl_ref, k, v):
    for index, operand in enumerate((k, k, v)):
        p_ref[index] = mm(wh_ref[index], operand, (1, 1)) + mm(wl_ref[index], operand, (1, 1))


def inner_kernel(rows, *refs):
    sources, rest = refs[:-7], refs[-7:]
    w_ref, out_ref, acc_ref, p_ref, x_ref, wh_ref, wl_ref = rest
    for index in range(3):
        wh_ref[index], wl_ref[index] = halves(w_ref[index])
    messages = pieces(sources[: len(sources) // 2], sources[len(sources) // 2 :])
    for step, group in groups_of(messages):
        put = functools.partial(add_to, acc_ref, out_ref, step)
        k, v = rows_of(group, 0, rows), rows_of(group, rows, rows)
        first_products(p_ref, wh_ref, wl_ref, k, v)
        forward_halves(p_ref, x_ref, rate_row(group, rows))
        for index, operand in enumerate((k, k, v)):
            put(index, mm(x_ref[2 * index], operand) + mm(x_ref[2 * index + 1], operand))


def outer_kernel(rows, *refs):
    layers = (len(refs) - 6) // 3
    messages, n_ref = pieces(refs[:layers], refs[layers : 2 * layers]), refs[2 * layers]
    gifts, rest = refs[2 * layers + 1 : -5], refs[-5:]
    out_ref, acc_ref, p_ref, x_ref, left_ref = rest
    gifts = pieces(gifts, gifts)
    hid = acc_ref.shape[1]
    parts = [whole(n_ref, index) for index in range(3)]
    for index in range(4):
        left_ref[:, index * hid : (index + 1) * hid] = parts[index // 2].T
    for (step, group), (_, back) in zip(groups_of(messages), groups_of(gifts)):
        put = functools.partial(add_to, acc_ref, out_ref, step)
        q, g = rows_of(group, 0, rows), rows_of(group, rows, rows)
        for index, operand in enumerate((q, q, g)):
            p_ref[index] = mm(parts[index], operand, (1, 1))
        forward_halves(p_ref, x_ref, None)
        stacked = x_ref[0:4].reshape(4 * hid, x_ref.shape[2])
        held = back
        give(held, mm(left_ref[...], stacked), 0, rows)
        for index, operand in enumerate((q, q, g)):
            put(index, mm(x_ref[2 * index], operand) + mm(x_ref[2 * index + 1], operand))


def second_halves(act_ref, p_ref, x_ref, r):
    def visit(at, columns):
        a, b, d = act_ref[(0, *at)], act_ref[(1, *at)], act_ref[(2, *at)]
        big_a, big_b, e = p_ref[(0, *at)], p_ref[(1, *at)], p_ref[(2, *at)]
        rate = r[:, columns]
        s = jax.nn.sigmoid(a)
        sa = a * s
        left = 1.0 - s
        ds = s * (1.0 + a * left)
        dds = s * left * (2.0 + a * (left - s))
        dh, er = d * rate, e * rate
        bds, dhds = b * ds, dh * ds
        hid = sa * b
        ddh = big_a * bds + big_b * sa
        put_halves(x_ref, 0, 1, at, dh * bds)
        put_halves(x_ref, 2, 3, at, dh * sa)
        put_halves(x_ref, 6, 4, at, er * bds + big_b * dhds + big_a * (dh * b * dds))
        put_halves(x_ref, 7, 5, at, er * sa + big_a * dhds)
        put_halves(x_ref, 8, 9, at, hid * rate)
        put_halves(x_ref, 11, 10, at, ddh * rate)
        return hid * e + ddh * d

    totals = by_blocks(p_ref.shape[1], p_ref.shape[2], visit)
    return jnp.concatenate([jnp.sum(t, axis=0, keepdims=True) for t in totals], axis=1)


def second_kernel(rows, *refs):
    layers = (len(refs) - 10) // 3
    sources = pieces(refs[:layers], refs[layers : 2 * layers])
    wh_ref, wl_ref, c_ref = refs[2 * layers : 2 * layers + 3]
    gifts, rest = refs[2 * layers + 3 : -7], refs[-7:]
    gifts = pieces(gifts, gifts)
    out_ref, acc_ref, act_ref, p_ref, x_ref = rest[:5]
    key_left, value_left = rest[5:]
    messages = sources
    hid = acc_ref.shape[1]
    parts = [whole(c_ref, index) for index in range(3)]
    gate, up, down = [part.T for part in parts]
    high, low = [wh_ref[index].T for index in range(3)], [wl_ref[index].T for index in range(3)]
    for left_ref, items in (
        (key_left, (gate, gate, up, up, high[0], high[1], high[0], high[1], low[0], low[1])),
        (value_left, (down, down, high[2], high[2], low[2])),
    ):
        for index, item in enumerate(items):
            left_ref[:, index * hid : (index + 1) * hid] = item
    for (step, group), (_, back) in zip(groups_of(messages), groups_of(gifts)):
        put = functools.partial(add_to, acc_ref, out_ref, step)
        k, v = rows_of(group, 0, rows), rows_of(group, rows, rows)
        for index, operand in enumerate((k, k, v)):
            p_ref[index] = mm(parts[index], operand, (1, 1))
        first_products(act_ref, wh_ref, wl_ref, k, v)
        d_rate = second_halves(act_ref, p_ref, x_ref, rate_row(group, rows))

        def stacked(first, last):
            return x_ref[first:last].reshape((last - first) * hid, x_ref.shape[2])

        dk = mm(key_left[:, : 8 * hid], stacked(0, 8)) + mm(key_left[:, 8 * hid :], stacked(6, 8))
        dv = mm(value_left[:, : 4 * hid], stacked(8, 12)) + mm(value_left[:, 4 * hid :], x_ref[11])
        held = back
        give(held, dk, 0, rows)
        give(held, dv, rows, rows)
        for slot, ref in enumerate(held):
            ref[2 * rows :] = padded_row(d_rate[:, slot * rows : (slot + 1) * rows], ref.shape[1])
        for index, (one, two, operand) in enumerate(((6, 4, k), (7, 5, k), (11, 10, v))):
            put(index, mm(x_ref[one], operand) + mm(x_ref[two], operand))


def total_of(in_ref):
    total = in_ref[0].astype(F32)
    for source in range(1, in_ref.shape[0]):
        total += in_ref[source].astype(F32)
    return total


def norm_of(rows):
    return jnp.sqrt(jnp.sum(rows * rows, axis=-1, keepdims=True) + EPSILON)


def spread(value, out_ref):
    rounded = value.astype(BF16)
    for owner in range(out_ref.shape[0]):
        out_ref[owner] = rounded


def update_kernel(in_ref, w_ref, out_ref, moved_ref):
    w = w_ref[...]
    moved = w + total_of(in_ref)
    moved_ref[...] = moved
    spread(moved * (norm_of(w) / norm_of(moved)), out_ref)


def back_kernel(in_ref, w_ref, moved_ref, out_ref, direct_ref):
    w, moved = w_ref[...], moved_ref[...]
    given = total_of(in_ref)
    old, new = norm_of(w), norm_of(moved)
    along = jnp.sum(given * moved, axis=-1, keepdims=True) / new
    cotangent = (given - moved * (along / new)) * (old / new)
    direct_ref[...] = cotangent + w * (along / old)
    spread(cotangent, out_ref)


def last_kernel(in_ref, direct_ref, out_ref):
    out_ref[...] = total_of(in_ref) + direct_ref[...]


def body(query_tokens, key_tokens, value_tokens, step_sizes, fast_weights, out_grad):
    rows = query_tokens.shape[0]
    layers, cores = lax.axis_size("z"), lax.axis_size("c")
    heads = layers * cores
    owners = lax.axis_size("p")
    width = query_tokens.shape[1] // heads
    hid = fast_weights.shape[2]
    share = hid // owners
    layer, place, core = lax.axis_index("z"), lax.axis_index("p"), lax.axis_index("c")
    product = 2 * heads * rows * hid * width
    shifts = [0, layers // 2] + [up for up in range(1, layers) if up != layers // 2]
    places = jnp.stack(
        [(layer + up) % layers * cores + (core + over) % cores for over in range(cores) for up in shifts]
    ).astype(jnp.int32)

    def along(messages, sign):
        pairs = [[(z, (z + sign * up) % layers) for z in range(layers)] for up in shifts]
        moved = [lax.ppermute(m, "z", pair) for m, pair in zip(messages[1:], pairs[1:])]
        return [messages[0]] + moved

    def across(messages):
        return [lax.ppermute(message, "c", [(0, 1), (1, 0)]) for message in messages]

    def scatter(message):
        message = message.reshape(owners, 3 * share, width)
        return lax.all_to_all(message, "p", 0, 0, tiled=True)

    weights = lax.dynamic_index_in_dim(fast_weights, core, 0, keepdims=False)
    own = lax.dynamic_slice_in_dim(weights, place * share, share, 1).reshape(3 * share, width)
    rounded = lax.reduce_precision(weights, 8, 7)
    w_high, w_low = rounded.astype(BF16), (weights - rounded).astype(BF16)
    memory = pl.BlockSpec(memory_space=pltpu.VMEM)
    scalars = pl.BlockSpec(memory_space=pltpu.SMEM)

    def messages_of(count):
        return (shape((cores * count, width), BF16),) * layers

    kv = along(
        call(
            pack_kv_kernel, messages_of(2 * rows + PAD), in_specs=[scalars, memory, memory, memory]
        )(places, key_tokens, value_tokens, step_sizes.T),
        1,
    )
    kv += across(kv)
    qg = along(
        call(pack_qg_kernel, messages_of(2 * rows), in_specs=[scalars, memory, memory])(
            places, query_tokens, out_grad
        ),
        1,
    )
    part_shape = shape((owners, 3, share, width), BF16)
    scratch = [pltpu.VMEM((3, hid, width), F32)]
    group_tokens = heads * rows // STEPS
    products = pltpu.VMEM((3, hid, group_tokens), F32)
    half_terms = pltpu.VMEM((6, hid, group_tokens), BF16)
    grad_part = call(
        functools.partial(inner_kernel, rows),
        part_shape,
        flops=12 * product,
        vmem=54,
        in_specs=[memory] * (heads + 1),
        out_specs=memory,
        scratch_shapes=scratch + [products, half_terms] + [pltpu.VMEM((3, hid, width), BF16)] * 2,
    )(*kv, weights)
    own_shape = shape((3 * share, width), F32)
    spread_shape = shape((owners, 3 * share, width), BF16)
    summed, qg[1] = lax.optimization_barrier((scatter(grad_part), qg[1]))
    updated, moved = call(update_kernel, (spread_shape, own_shape))(summed, own)
    updated, got = lax.optimization_barrier((scatter(updated), across(qg)))
    updated, qg = updated.reshape(owners, 3, share, width), qg + got
    *d_queries, d_part = call(
        functools.partial(outer_kernel, rows),
        messages_of(rows) + (part_shape,),
        flops=13 * product,
        vmem=54,
        in_specs=[memory] * (heads + 1),
        out_specs=[memory] * (layers + 1),
        scratch_shapes=scratch
        + [
            products,
            half_terms,
            pltpu.VMEM((width, 4 * hid), BF16),
        ],
    )(*qg, updated)
    given, d_queries = lax.optimization_barrier((scatter(d_part), along(d_queries, -1)))
    cotangent, direct = call(back_kernel, (spread_shape, own_shape))(given, own, moved)
    wide = (rows, heads * width)
    taken = [scalars] + [memory] * heads
    query_grad = call(unpack_q_kernel, shape(wide, BF16), in_specs=taken)(
        places, *d_queries, *across(d_queries)
    )
    cotangent, query_grad = lax.optimization_barrier((scatter(cotangent), query_grad))
    cotangent = cotangent.reshape(owners, 3, share, width)
    *d_kv, second_part = call(
        functools.partial(second_kernel, rows),
        messages_of(2 * rows + PAD) + (part_shape,),
        flops=24 * product,
        vmem=54,
        in_specs=[memory] * (heads + 3),
        out_specs=[memory] * (layers + 1),
        scratch_shapes=scratch
        + [
            products,
            products,
            pltpu.VMEM((12, hid, group_tokens), BF16),
            pltpu.VMEM((width, 10 * hid), BF16),
            pltpu.VMEM((width, 5 * hid), BF16),
        ],
    )(*kv, w_high, w_low, cotangent)
    d_kv = along(d_kv, -1)
    summed = call(last_kernel, own_shape)(scatter(second_part), direct)
    summed = summed.reshape(3, 2, share // 2, width)
    kept = lax.dynamic_index_in_dim(summed, core, 1, keepdims=False)
    sent = lax.dynamic_index_in_dim(summed, 1 - core, 1, keepdims=False)
    got = lax.ppermute(sent, "c", [(0, 1), (1, 0)])
    first = core == 0
    meta_grad = jnp.stack([jnp.where(first, kept, got), jnp.where(first, got, kept)])
    got, meta_grad = lax.optimization_barrier((across(d_kv), meta_grad))
    key_grad, value_grad, step_grad = call(
        unpack_kv_kernel,
        (shape(wide, BF16), shape(wide, BF16), shape((heads, rows), BF16)),
        in_specs=taken,
    )(places, *d_kv, *got)
    step_grad = step_grad.T
    return meta_grad, query_grad, key_grad, value_grad, step_grad


def solution(mesh):
    layers, lines = mesh.devices.shape
    small = Mesh(mesh.devices.reshape(layers, lines // 2, 2), ("z", "p", "c"))
    rows = P(("z", "p", "c"), None)
    return jax.shard_map(
        body,
        mesh=small,
        in_specs=(rows, rows, rows, rows, P("z", None, None, None), rows),
        out_specs=(P("z", None, ("p", "c"), None), rows, rows, rows, rows),
        check_vma=False,
    )
```
